256 devices in a mesh: group: 4 (over x_hi, core), fsdp: 64 (over z, y, x_lo).
Axes of the slice: x: 4 (x_hi: 2, x_lo: 2; x = x_hi * 2 + x_lo), y: 4, z: 8, core: 2. Of those that a mesh axis runs over, the one named last changes fastest.
Arguments:
- tokens: bfloat16 [4, 16384, 2048], P('group', 'fsdp'), may hold values from -16 to 16
- targets: bfloat16 [4, 16384, 1024], P('group', 'fsdp'), may hold values from -6 to 6
- lengths: int32 [4, 64], P('group'), may hold values from 128 to 256, as said below
- outer_param: float32 [2048, 1024], P('fsdp', 'group'), may hold values from -6 to 6
- outer_mom: float32 [2048, 1024], P('fsdp', 'group'), may hold values from -0.75 to 0.75
- first_mom: float32 [4, 2048, 1024], P('group', 'fsdp'), may hold values from -0.0014648438 to 0.0014648438
- second_mom: float32 [4, 2048, 1024], P('group', 'fsdp'), may hold values from 5e-09 to 5e-08
Outputs:
- new_param: float32 [2048, 1024], P('fsdp', 'group')
- new_mom: float32 [2048, 1024], P('fsdp', 'group')
- new_first: float32 [4, 2048, 1024], P('group', 'fsdp')
- new_second: float32 [4, 2048, 1024], P('group', 'fsdp')
The draws below stay inside these ranges and needn't reach their ends.
Inputs may be any that keep to these rules, and one draw needn't show every extreme that they name: `lengths`: every entry is a multiple of 128, and some entry equals 256.
All inputs are finite; a program needn't handle non-finite values.
Results may differ from the reference program's by a relative error of at most 0.0075.
Values may be sent and summed in bfloat16 or wider, within the bound.
No kernel may reach another device: no remote copies, remote signals or barrier semaphores. Data moves between devices by JAX's collectives and lax.ppermute only.
A program may use at most 64 MiB of HBM per device.

```python
import math
import jax
import jax.numpy as jnp
from jax import lax

D = 2048
KV = 1024
TOK_DEV = 256
STEPS = 2
PRIOR = 1000
GROUPS = 4
TOKENS = 16384


def draw_lengths(key, part):
    key = jax.random.fold_in(key, 11)
    blocks_key, pick_key = jax.random.split(key)
    most = TOK_DEV // 128
    members = TOKENS // TOK_DEV
    blocks = jax.random.randint(blocks_key, (GROUPS * members,), 1, most + 1)
    chosen = jax.random.randint(pick_key, (), 0, GROUPS * members)
    blocks = jnp.where(jnp.arange(GROUPS * members) == chosen, most, blocks)
    return (blocks * 128).astype(jnp.int32).reshape(GROUPS, members)


def strengthened(drawn, own_key, source, target, blocks, factor):
    def block_of(axis_at):
        return (jnp.arange(drawn.shape[axis_at]) // (drawn.shape[axis_at] // blocks)).reshape((-1,) + (1,) * (drawn.ndim - 1 - axis_at))

    near = jax.random.permutation(own_key, blocks)[block_of(target)]
    far = (block_of(target) + blocks // 2) % blocks
    return jnp.where((block_of(source) == near) | (block_of(source) == far), factor * drawn, drawn)


def steps_of(stream_key, extent, pieces, low, largest):
    gain = 1.0
    for axis_at, shards_of in pieces:
        steps = jax.random.uniform(jax.random.fold_in(jax.random.fold_in(stream_key, 6), axis_at), (shards_of,), jnp.float32, low / len(pieces), largest / len(pieces))
        gain = gain * jnp.repeat(jnp.exp(steps), extent[axis_at] // shards_of).reshape((-1,) + (1,) * (len(extent) - 1 - axis_at))
    return gain


def scatter_about(own_key, extent, spread, limit, cuts=(), kind=jnp.bfloat16):
    drawn = jax.random.normal(own_key, extent, jnp.float32) * spread
    if len(cuts) > 0:
        drawn = steps_of(own_key, extent, cuts, -0.22, 0.18) * drawn
    return jnp.clip(drawn, min=-limit, max=limit).astype(kind)


def heavy_noise(rng, shape, scale, limit, cuts, heavy, held_as=jnp.bfloat16):
    drawn = scale * jax.random.normal(rng, shape, jnp.float32)
    if cuts:
        drawn = drawn * steps_of(rng, shape, cuts, -0.22, 0.18)
    return jnp.clip(strengthened(drawn, jax.random.fold_in(rng, 3), *heavy), -limit, limit).astype(held_as)


def setup_inputs(seed: int = 0) -> dict:
    keys = jax.random.split(jax.random.key(seed), 8)
    tokens = heavy_noise(keys[0], (GROUPS, TOKENS, D), 1.0, 16.0, ((0, 4), (1, 64)), (1, 2, 64, 4.0))
    targets = scatter_about(keys[1], (GROUPS, TOKENS, KV), 1.0, 6.0, ((0, 4), (1, 64)))
    lengths = draw_lengths(jax.random.fold_in(keys[7], 71), 0)
    outer_param = scatter_about(keys[3], (D, KV), 1.0, 6.0, ((0, 64), (1, 4)), jnp.float32)
    outer_mom = scatter_about(keys[4], (D, KV), 0.05, 0.75, ((0, 64), (1, 4)), jnp.float32)
    first_mom = scatter_about(keys[5], (GROUPS, D, KV), 0.0001, 0.0014648438, ((0, 4), (1, 64)), jnp.float32)
    second_mom = jnp.clip(jnp.exp(math.log(5.000000058430487e-08) - 2.3025851 * jax.random.uniform(keys[6], (GROUPS, D, KV), jnp.float32) ** steps_of(keys[6], (GROUPS, D, KV), ((0, 4), (1, 64)), -0.2, 0.2)), 4.999999969612645e-09, 5.000000058430487e-08)
    return dict(tokens=tokens, targets=targets, lengths=lengths, outer_param=outer_param, outer_mom=outer_mom, first_mom=first_mom, second_mom=second_mom)


def adam_update(param, first, second, grad, step):
    first = 0.9 * first + 0.1 * grad
    second = 0.95 * second + 0.05 * grad * grad
    upd = first / (1.0 - 0.9 ** step) / (jnp.sqrt(second / (1.0 - 0.95 ** step)) + 1e-08)
    return (param - 0.1 * (upd + 0.1 * param), first, second)

def group_gradient(inputs, goal, valid, param, count):
    factor = D ** (-0.5)
    weights = param.astype(jnp.bfloat16)
    outputs = jnp.dot(inputs, weights, preferred_element_type=jnp.float32) * factor
    resid = (valid * (outputs - goal.astype(jnp.float32))).astype(jnp.bfloat16)
    total = lax.dot_general(inputs, resid, (((0,), (0,)), ((), ())), preferred_element_type=jnp.float32)
    return total * (factor / count)

def reference(tokens, targets, lengths, outer_param, outer_mom, first_mom, second_mom):
    rows = jnp.arange(TOKENS, dtype=jnp.int32)
    row_local = rows % TOK_DEV
    row_owner = rows // TOK_DEV
    change = jnp.zeros((D, KV), jnp.float32)
    firsts = []
    seconds = []
    for group in range(GROUPS):
        limits = lengths[group][row_owner]
        valid = (row_local < limits).astype(jnp.float32)[:, None]
        count = jnp.sum(lengths[group]).astype(jnp.float32)
        param = outer_param
        first = first_mom[group]
        second = second_mom[group]
        for step in range(STEPS):
            grad = group_gradient(tokens[group], targets[group], valid, param, count)
            param, first, second = adam_update(param, first, second, grad, PRIOR + step + 1)
        change = change + (outer_param - param)
        firsts.append(first)
        seconds.append(second)
    pseudo = change / GROUPS
    new_mom = 0.9 * outer_mom + pseudo
    new_param = outer_param - 0.7 * (pseudo + 0.9 * new_mom)
    return (new_param, new_mom, jnp.stack(firsts), jnp.stack(seconds))
```

```python
import jax
import jax.numpy as jnp
from jax import lax
from jax.sharding import Mesh
from jax.sharding import PartitionSpec as P

D = 2048
STEPS = 2
PRIOR = 1000
BLOCK = 128
TURN = [(0, 0), (1, 2), (2, 1), (3, 3)]


def adam_moments(first, second, grad):
    return 0.9 * first + 0.1 * grad, 0.95 * second + 0.05 * grad * grad


def adam_update(param, first, second, step):
    upd = first / (1.0 - 0.9**step) / (jnp.sqrt(second / (1.0 - 0.95**step)) + 1e-08)
    return param - 0.1 * (upd + 0.1 * param)


def shift(x, axis, by):
    size = lax.axis_size(axis)
    return lax.ppermute(x, axis, [(i, (i + by) % size) for i in range(size)])


def other_core(x):
    return shift(x, "c", 1)


def exchange(x, axes):
    return lax.all_to_all(x, axes, 0, 0, tiled=True)


def pick(x, index, axis):
    return lax.dynamic_index_in_dim(x, index, axis, keepdims=False)


def turned(x):
    return lax.ppermute(x, ("c", "x"), TURN)


def spread_rows(x):
    own = turned(x)
    half = own.shape[0] // 2
    above = shift(own, ("yh", "yl"), -1)
    below = shift(own, ("yh", "yl"), 1)
    far = jnp.concatenate(
        [shift(above[:half], ("yh", "yl"), -1), shift(below[half:], ("yh", "yl"), 1)], 0
    )
    return [(0, own), (1, above), (3, below), (2, far)]


def per_device(tokens, targets, lengths, outer_param, outer_mom, first_mom, second_mom):
    c, x = lax.axis_index("c"), lax.axis_index("x")
    z, h = lax.axis_index("z"), lax.axis_index("h")
    y, yh = lax.axis_index(("yh", "yl")), lax.axis_index("yh")
    rows = tokens.shape[1]
    factor = D ** (-0.5)

    sizes = turned(lengths[0])
    coef = factor / jnp.sum(sizes).astype(jnp.float32)
    goals = lax.all_to_all(turned(targets[0]), ("yh", "c", "yl"), 1, 0, tiled=True)
    goals = goals.reshape(2, 2, 2, rows, BLOCK)
    blocks, wanted, valid = [], [], []
    for away, block in spread_rows(tokens[0]):
        for core, part in ((c, block), (1 - c, other_core(block))):
            at = (y + away) % 4
            blocks.append(part)
            goal = pick(pick(pick(goals, at // 2, 0), core, 0), at % 2, 0)
            wanted.append(goal)
            limit = pick(sizes, (z * 4 + at) * 2 + core, 0)
            valid.append((lax.iota(jnp.int32, rows) < limit).astype(jnp.float32))
    inputs = jnp.concatenate(blocks, 0)
    goal = jnp.concatenate(wanted, 0)
    valid = jnp.concatenate(valid, 0)[:, None]

    param = jnp.moveaxis(outer_param.reshape(32, 2, BLOCK), 1, 0)
    param = jnp.broadcast_to(param[None, None, :, None], (2, 2, 2, 2, 32, BLOCK))
    param = exchange(param.reshape(16, 32, BLOCK), ("h", "yh", "yl", "x"))
    param = pick(param.reshape(2, 256, BLOCK), yh, 0)
    moments = jnp.stack([first_mom[0], second_mom[0]]).reshape(2, 32, 2, 2, 2, BLOCK)
    moments = moments.transpose(3, 2, 4, 0, 1, 5)[:, :, :, None]
    moments = jnp.broadcast_to(moments, (2, 2, 2, 2, 2, 32, BLOCK))
    moments = exchange(moments.reshape(16, 2, 32, BLOCK), ("c", "yh", "yl", "x"))
    moments = pick(moments.reshape(2, 8, 2, 32, BLOCK), x, 0)
    first = moments[:, 0].reshape(256, BLOCK)
    second = moments[:, 1].reshape(256, BLOCK)

    start = param
    home_first, home_second = first_mom[0], second_mom[0]
    for step in range(STEPS):
        weights = jnp.broadcast_to(param.astype(jnp.bfloat16)[None], (8, 256, BLOCK))
        weights = exchange(weights, "z").reshape(D, BLOCK)
        outputs = jnp.dot(inputs, weights, preferred_element_type=jnp.float32) * factor
        resid = (valid * (outputs - goal.astype(jnp.float32))).astype(jnp.bfloat16)
        grad = lax.dot_general(
            inputs, resid, (((0,), (0,)), ((), ())), preferred_element_type=jnp.float32
        )
        grad = exchange(grad.astype(jnp.bfloat16).reshape(8, 256, BLOCK), "z")
        grad = jnp.sum(grad.astype(jnp.float32), 0) * coef
        first, second = adam_moments(first, second, grad)
        param = adam_update(param, first, second, PRIOR + step + 1)

        home = grad.astype(jnp.bfloat16).reshape(1, 8, 32, BLOCK)
        home = jnp.broadcast_to(home, (2, 8, 32, BLOCK)).reshape(16, 32, BLOCK)
        home = exchange(home, ("c", "yh", "yl", "x"))
        home = pick(home.reshape(2, 2, 2, 2, 32, BLOCK), c, 3)
        home = home.transpose(3, 1, 0, 2, 4).reshape(32, 8 * BLOCK)
        home_first, home_second = adam_moments(
            home_first, home_second, home.astype(jnp.float32)
        )

    change = (start - param).astype(jnp.bfloat16).reshape(1, 8, 32, BLOCK)
    change = jnp.broadcast_to(change, (2, 8, 32, BLOCK)).reshape(16, 32, BLOCK)
    change = exchange(change, ("h", "yh", "yl", "x")).reshape(2, 2, 2, 2, 32, BLOCK)
    change = jnp.sum(pick(change, h, 1).astype(jnp.float32), (0, 2))
    pseudo = jnp.moveaxis(change, 0, 1).reshape(32, 2 * BLOCK) / 4
    new_mom = 0.9 * outer_mom + pseudo
    new_param = outer_param - 0.7 * (pseudo + 0.9 * new_mom)
    return (new_param, new_mom, home_first[None], home_second[None])


def solution(mesh):
    fine = Mesh(
        mesh.devices.reshape(2, 2, 8, 2, 2, 2), ("h", "c", "z", "yh", "yl", "x")
    )
    group, fsdp = ("h", "c"), ("z", "yh", "yl", "x")
    in_specs = (
        P(group, fsdp, None),
        P(group, fsdp, None),
        P(group, None),
        P(fsdp, group),
        P(fsdp, group),
        P(group, fsdp, None),
        P(group, fsdp, None),
    )
    out_specs = (
        P(fsdp, group),
        P(fsdp, group),
        P(group, fsdp, None),
        P(group, fsdp, None),
    )
    return jax.shard_map(
        per_device, mesh=fine, in_specs=in_specs, out_specs=out_specs, check_vma=False
    )
```

```python
import functools

import jax
import jax.numpy as jnp
from jax import lax
from jax.experimental import pallas as pl
from jax.experimental.pallas import tpu as pltpu
from jax.sharding import Mesh
from jax.sharding import PartitionSpec as P

D = 2048
STEPS = 2
PRIOR = 1000
BLOCK = 128
FIRST = 64
TURN = [(0, 0), (1, 2), (2, 1), (3, 3)]

OWN = ((0, FIRST, 256),)
LEAD = ((0, 0, FIRST), (1, 0, FIRST), (3, 0, FIRST), (2, 0, FIRST))
ABOVE = ((1, FIRST, 256),)
BELOW = ((3, FIRST, 256),)
FAR = ((2, FIRST, 128), (2, 128, 256))


def adam_moments(first, second, grad):
    return 0.9 * first + 0.1 * grad, 0.95 * second + 0.05 * grad * grad


def adam_update(param, first, second, step):
    upd = first / (1.0 - 0.9**step) / (jnp.sqrt(second / (1.0 - 0.95**step)) + 1e-08)
    return param - 0.1 * (upd + 0.1 * param)


def shift(x, axis, by):
    size = lax.axis_size(axis)
    return lax.ppermute(x, axis, [(i, (i + by) % size) for i in range(size)])


def other_core(x):
    return shift(x, "c", 1)


def exchange(x, axes):
    return lax.all_to_all(x, axes, 0, 0, tiled=True)


def pick(x, index, axis):
    return lax.dynamic_index_in_dim(x, index, axis, keepdims=False)


def after(x, *earlier):
    return lax.optimization_barrier((x, *earlier))[0]


def turned(x):
    return lax.ppermute(x, ("c", "x"), TURN)


def up(x):
    return shift(x, ("yh", "yl"), 1)


def down(x):
    return shift(x, ("yh", "yl"), -1)


def product_kernel(chunks, last, place, goals, weights, *refs):
    count = sum(len(blocks) for blocks, _ in chunks)
    blocks, refs = refs[:count], refs[count:]
    earlier, out, held, total, sems = refs if len(refs) == 5 else (None, *refs)
    copies, row = [], 0
    for at, block in enumerate(blocks):
        rows = block.shape[0]
        copy = pltpu.make_async_copy(block, held.at[pl.ds(row, rows)], sems.at[at])
        copy.start()
        copies.append(copy)
        row += rows
    if earlier is not None:
        total[...] = earlier[...]
    row = done = 0
    for number, (parts, rows_of) in enumerate(chunks):
        goal = []
        for core in range(2):
            for away, low, high in rows_of:
                source = lax.rem(place[0] + away, 4) * 2 + lax.rem(place[1] + core, 2)
                goal.append(goals[source, low:high])
        goal = jnp.concatenate(goal, 0).astype(jnp.float32)
        for copy in copies[done : done + len(parts)]:
            copy.wait()
        done += len(parts)
        inputs = held[row : row + goal.shape[0]]
        row += goal.shape[0]
        outputs = jnp.dot(inputs, weights[...], preferred_element_type=jnp.float32)
        resid = (outputs * D ** (-0.5) - goal).astype(jnp.bfloat16)
        grad = lax.dot_general(
            resid, inputs, (((0,), (0,)), ((), ())), preferred_element_type=jnp.float32
        )
        if number == 0 and earlier is None:
            total[...] = grad
        else:
            total[...] += grad
    if last:
        for z in range(8):
            out[z] = total[:, z * 256 : (z + 1) * 256].T.astype(jnp.bfloat16)
    else:
        out[...] = total[...]


def product(chunks, place, goals, weights, earlier=None, last=False):
    blocks = [block for parts, _ in chunks for block in parts]
    rows = sum(block.shape[0] for block in blocks)
    whole = pl.BlockSpec(memory_space=pltpu.VMEM)
    args = [place, goals, weights, *blocks]
    specs = [pl.BlockSpec(memory_space=pltpu.SMEM), whole, whole]
    specs += [pl.BlockSpec(memory_space=pl.ANY)] * len(blocks)
    if earlier is not None:
        args.append(earlier)
        specs.append(whole)
    shape = ((8, 256, BLOCK), jnp.bfloat16) if last else ((BLOCK, D), jnp.float32)
    return pl.pallas_call(
        functools.partial(product_kernel, [(len(p) * [0], r) for p, r in chunks], last),
        out_shape=jax.ShapeDtypeStruct(*shape),
        in_specs=specs,
        out_specs=whole,
        scratch_shapes=[
            pltpu.VMEM((rows, D), jnp.bfloat16),
            pltpu.VMEM((BLOCK, D), jnp.float32),
            pltpu.SemaphoreType.DMA((len(blocks),)),
        ],
        compiler_params=pltpu.CompilerParams(vmem_limit_bytes=40 * 2**20),
        cost_estimate=pl.CostEstimate(
            flops=8 * rows * D * BLOCK, bytes_accessed=2 * rows * D, transcendentals=0
        ),
    )(*args)


def gathered(param):
    weights = jnp.broadcast_to(param.astype(jnp.bfloat16)[None], (8, 256, BLOCK))
    return exchange(weights, "z").reshape(D, BLOCK)


def reduced(grad):
    return jnp.sum(exchange(grad, "z").astype(jnp.float32), 0)


def per_device(tokens, targets, lengths, outer_param, outer_mom, first_mom, second_mom):
    c, x = lax.axis_index("c"), lax.axis_index("x")
    h, y, yh = lax.axis_index("h"), lax.axis_index(("yh", "yl")), lax.axis_index("yh")
    place = jnp.stack([y, c]).astype(jnp.int32)

    own = lax.axis_index(("z", "yh", "yl", "x"))
    valid = lax.iota(jnp.int32, tokens.shape[1]) < pick(lengths[0], own, 0)
    masked = jnp.where(valid[:, None], tokens[0], jnp.zeros((), tokens.dtype))
    lead, rest = masked[:FIRST], masked[FIRST:]

    rest = turned(rest)
    lead_above, lead_below = down(lead), up(lead)

    start = jnp.moveaxis(outer_param.reshape(32, 2, BLOCK), 1, 0)
    start = jnp.broadcast_to(start[None, None, :, None], (2, 2, 2, 2, 32, BLOCK))
    start = exchange(start.reshape(16, 32, BLOCK), ("h", "yh", "yl", "x"))

    lead_far = down(lead_above)
    above, below = down(rest), up(rest)
    lead = turned(jnp.concatenate([lead, lead_above, lead_below, lead_far], 0))

    goals = after(targets[0], rest).reshape(256, 2, 2, 2, BLOCK)
    goals = turned(goals.transpose(1, 3, 2, 0, 4).reshape(8, 256, BLOCK))
    goals = exchange(goals, ("yh", "yl", "c"))
    start = pick(start.reshape(2, 256, BLOCK), yh, 0)
    weights = gathered(start)

    far_a, far_b = down(above[:FIRST]), up(below[FIRST:])
    chunks = [
        ((rest, other_core(rest)), OWN),
        ((lead, other_core(lead)), LEAD),
        ((above, other_core(above)), ABOVE),
        ((below, other_core(below)), BELOW),
        ((far_a, far_b, other_core(far_a), other_core(far_b)), FAR),
    ]
    grad = product(chunks[:2], place, goals, weights)
    grad = product(chunks[2:4], place, goals, weights, grad)
    grad = product(chunks[4:], place, goals, weights, grad, last=True)

    moments = jnp.stack([first_mom[0], second_mom[0]])
    moments = after(moments, grad)
    moments = moments.reshape(2, 32, 2, 2, 2, BLOCK)
    moments = moments.transpose(3, 2, 4, 0, 1, 5)[:, :, :, None]
    moments = jnp.broadcast_to(moments, (2, 2, 2, 2, 2, 32, BLOCK))
    moments = exchange(moments.reshape(16, 2, 32, BLOCK), ("c", "yh", "yl", "x"))
    moments = pick(moments.reshape(2, 8, 2, 32, BLOCK), x, 0)
    first = moments[:, 0].reshape(256, BLOCK)
    second = moments[:, 1].reshape(256, BLOCK)

    count = jnp.sum(lengths[0]).astype(jnp.float32).reshape(1)
    count = jnp.where(c == x, count, other_core(count))
    coef = D ** (-0.5) / count

    grad = reduced(grad) * coef
    grads = [grad.astype(jnp.bfloat16)]
    first, second = adam_moments(first, second, grad)
    param = adam_update(start, first, second, PRIOR + 1)

    grad = product(chunks, place, goals, gathered(param), last=True)
    grad = reduced(grad) * coef
    grads.append(grad.astype(jnp.bfloat16))
    first, second = adam_moments(first, second, grad)
    param = adam_update(param, first, second, PRIOR + 2)

    change = (start - param).astype(jnp.bfloat16).reshape(1, 8, 32, BLOCK)
    change = jnp.broadcast_to(change, (2, 8, 32, BLOCK)).reshape(16, 32, BLOCK)
    change = exchange(change, ("h", "yh", "yl", "x")).reshape(2, 2, 2, 2, 32, BLOCK)
    change = jnp.sum(pick(change, h, 1).astype(jnp.float32), (0, 2))
    pseudo = jnp.moveaxis(change, 0, 1).reshape(32, 2 * BLOCK) / 4
    new_mom = 0.9 * outer_mom + pseudo
    new_param = outer_param - 0.7 * (pseudo + 0.9 * new_mom)

    home = jnp.stack([grad.reshape(8, 32, BLOCK) for grad in grads], 1)[None]
    home = jnp.broadcast_to(home, (2, 8, 2, 32, BLOCK)).reshape(16, 2, 32, BLOCK)
    home = exchange(home, ("c", "yh", "yl", "x"))
    home = pick(home.reshape(2, 2, 2, 2, 2, 32, BLOCK), c, 3)
    home = home.transpose(3, 4, 1, 0, 2, 5).reshape(2, 32, 8 * BLOCK)
    first, second = first_mom[0], second_mom[0]
    for step in range(STEPS):
        first, second = adam_moments(first, second, home[step].astype(jnp.float32))
    return (new_param, new_mom, first[None], second[None])


def solution(mesh):
    fine = Mesh(
        mesh.devices.reshape(2, 2, 8, 2, 2, 2), ("h", "c", "z", "yh", "yl", "x")
    )
    group, fsdp = ("h", "c"), ("z", "yh", "yl", "x")
    in_specs = (
        P(group, fsdp, None),
        P(group, fsdp, None),
        P(group, None),
        P(fsdp, group),
        P(fsdp, group),
        P(group, fsdp, None),
        P(group, fsdp, None),
    )
    out_specs = (
        P(fsdp, group),
        P(fsdp, group),
        P(group, fsdp, None),
        P(group, fsdp, None),
    )
    return jax.shard_map(
        per_device, mesh=fine, in_specs=in_specs, out_specs=out_specs, check_vma=False
    )
```

```python
import functools

import jax
import jax.numpy as jnp
from jax import lax
from jax.experimental import pallas as pl
from jax.experimental.pallas import tpu as pltpu
from jax.sharding import Mesh
from jax.sharding import PartitionSpec as P

D = 2048
STEPS = 2
PRIOR = 1000
BLOCK = 128
TURN = [(0, 0), (1, 2), (2, 1), (3, 3)]
WIDE = 2 * BLOCK
PEERS = [[z * 4 + (colour + 2 * z) % 4 for z in range(8)] for colour in range(4)]


def adam_moments(first, second, grad):
    return 0.9 * first + 0.1 * grad, 0.95 * second + 0.05 * grad * grad


def adam_update(param, first, second, step):
    upd = first / (1.0 - 0.9**step) / (jnp.sqrt(second / (1.0 - 0.95**step)) + 1e-08)
    return param - 0.1 * (upd + 0.1 * param)


def shift(x, axis, by):
    size = lax.axis_size(axis)
    return lax.ppermute(x, axis, [(i, (i + by) % size) for i in range(size)])


def other_core(x):
    return shift(x, "c", 1)


def exchange(x, axes):
    return lax.all_to_all(x, axes, 0, 0, tiled=True)


def pick(x, index, axis):
    return lax.dynamic_index_in_dim(x, index, axis, keepdims=False)


def after(x, *earlier):
    return lax.optimization_barrier((x, *earlier))[0]


def turned(x):
    return lax.ppermute(x, ("c", "x"), TURN)


def up(x):
    return shift(x, ("yh", "yl"), 1)


def down(x):
    return shift(x, ("yh", "yl"), -1)


def product_kernel(layout, last, core, weights, *refs):
    count = len(layout)
    blocks, refs = refs[:count], refs[count:]
    earlier, out, held, goals, total, sems = refs if len(refs) == 6 else (None, *refs)
    copies, row = [], 0
    for at, (rows, inputs_at, goals_at) in enumerate(layout):
        half = pl.multiple_of(goals_at + core[0] * BLOCK, BLOCK)
        sources = blocks[at].at[:, pl.ds(inputs_at, D)], blocks[at].at[:, pl.ds(half, BLOCK)]
        here = pl.ds(row, rows)
        for kind, (source, target) in enumerate(zip(sources, (held, goals))):
            copy = pltpu.make_async_copy(source, target.at[here], sems.at[kind, at])
            copy.start()
            copies.append(copy)
        row += rows
    if earlier is not None:
        total[...] = earlier[...]
    row = at = 0
    while at < count:
        size = 0
        while size < 512:
            copies[2 * at].wait()
            copies[2 * at + 1].wait()
            size += layout[at][0]
            at += 1
        inputs = held[row : row + size]
        goal = goals[row : row + size].astype(jnp.float32)
        outputs = jnp.dot(inputs, weights[...], preferred_element_type=jnp.float32)
        resid = (outputs * D ** (-0.5) - goal).astype(jnp.bfloat16)
        grad = lax.dot_general(
            resid, inputs, (((0,), (0,)), ((), ())), preferred_element_type=jnp.float32
        )
        if row == 0 and earlier is None:
            total[...] = grad
        else:
            total[...] += grad
        row += size
    if last:
        for z in range(8):
            out[z] = total[:, z * 256 : (z + 1) * 256].T.astype(jnp.bfloat16)
    else:
        out[...] = total[...]


def product(parts, core, weights, earlier=None, last=False):
    blocks = [block for block, _, _ in parts]
    layout = [(block.shape[0], *places) for block, *places in parts]
    rows = sum(block.shape[0] for block in blocks)
    whole = pl.BlockSpec(memory_space=pltpu.VMEM)
    args = [core, weights, *blocks]
    specs = [pl.BlockSpec(memory_space=pltpu.SMEM), whole]
    specs += [pl.BlockSpec(memory_space=pl.ANY)] * len(blocks)
    if earlier is not None:
        args.append(earlier)
        specs.append(whole)
    shape = ((8, 256, BLOCK), jnp.bfloat16) if last else ((BLOCK, D), jnp.float32)
    return pl.pallas_call(
        functools.partial(product_kernel, layout, last),
        out_shape=jax.ShapeDtypeStruct(*shape),
        in_specs=specs,
        out_specs=whole,
        scratch_shapes=[
            pltpu.VMEM((rows, D), jnp.bfloat16),
            pltpu.VMEM((rows, BLOCK), jnp.bfloat16),
            pltpu.VMEM((BLOCK, D), jnp.float32),
            pltpu.SemaphoreType.DMA((2, len(blocks))),
        ],
        compiler_params=pltpu.CompilerParams(vmem_limit_bytes=40 * 2**20),
        cost_estimate=pl.CostEstimate(
            flops=8 * rows * D * BLOCK, bytes_accessed=2 * rows * D, transcendentals=0
        ),
    )(*args)


def among_peers(x):
    axes = ("z", "yh", "yl")
    return lax.all_to_all(x, axes, 0, 0, axis_index_groups=PEERS, tiled=True)


def gathered(param):
    weights = jnp.broadcast_to(param.astype(jnp.bfloat16)[None], (8, 256, BLOCK))
    return among_peers(weights).reshape(D, BLOCK)


def reduced(grad):
    return jnp.sum(among_peers(grad).astype(jnp.float32), 0)


def per_device(tokens, targets, lengths, outer_param, outer_mom, first_mom, second_mom):
    c, x, z = (lax.axis_index(axis) for axis in ("c", "x", "z"))
    h, y = lax.axis_index("h"), lax.axis_index(("yh", "yl"))
    odd = z % 2
    colour = (y + 2 * odd) % 4
    core = c.reshape(1).astype(jnp.int32)

    own = lax.axis_index(("z", "yh", "yl", "x"))
    valid = lax.iota(jnp.int32, tokens.shape[1]) < pick(lengths[0], own, 0)
    masked = jnp.where(valid[:, None], tokens[0], jnp.zeros((), tokens.dtype))

    goals = targets[0].reshape(256, 2, 2, 2, BLOCK).transpose(1, 3, 0, 2, 4)
    goals = goals.reshape(4, 256, WIDE)
    goals = [pick(goals, (colour + away) % 4, 0) for away in range(4)]
    mine = jnp.concatenate([goals[1], masked, goals[3], goals[2], goals[0]], 1)
    mine = turned(mine)
    from_below = up(mine[:, : D + WIDE])
    from_above = down(mine[:, WIDE : D + 2 * WIDE])
    half = mine.shape[0] // 2
    before = shift(mine[:half, WIDE : D + 3 * WIDE], "z", 1)
    behind = shift(mine[half:, WIDE : D + 3 * WIDE], "z", -1)

    start = jnp.moveaxis(outer_param.astype(jnp.bfloat16).reshape(32, 2, BLOCK), 1, 0)
    start = jnp.broadcast_to(start[None, None, :, None], (2, 2, 2, 2, 32, BLOCK))
    start = exchange(start.reshape(16, 32, BLOCK), ("h", "yh", "yl", "x"))
    start = start.reshape(2, 256, BLOCK)
    here = pick(start, colour // 2, 0)
    there = pick(start, 1 - colour // 2, 0)
    weights = jnp.where(
        (jnp.arange(8) % 2 == odd)[:, None, None], here[None], there[None]
    )
    weights = exchange(weights, "z").reshape(D, BLOCK)
    start = here.astype(jnp.float32)

    count = (jnp.sum(lengths[0]) // 128).astype(jnp.bfloat16)
    moments = jnp.concatenate([first_mom[0], second_mom[0]], 0).astype(jnp.bfloat16)
    moments = moments.reshape(64, 2, 2, 2, BLOCK)
    moments = jnp.where(odd == 1, moments[:, ::-1], moments).transpose(2, 1, 3, 0, 4)
    moments = jnp.concatenate(
        [moments, jnp.broadcast_to(count, (2, 2, 2, 16, BLOCK))], 3
    )
    moments = jnp.broadcast_to(moments[:, :, :, None], (2, 2, 2, 2, 80, BLOCK))
    moments = exchange(
        after(moments.reshape(16, 80, BLOCK), mine), ("c", "yh", "yl", "x")
    )
    moments = pick(moments.reshape(2, 8, 80, BLOCK), x, 0)
    weights, moments = lax.optimization_barrier((weights, moments))
    first = moments[:, :32].reshape(256, BLOCK).astype(jnp.float32)
    second = moments[:, 32:64].reshape(256, BLOCK).astype(jnp.float32)
    coef = D ** (-0.5) / (128.0 * moments[0, 64, 0].astype(jnp.float32))

    near = [(block, WIDE, D + 3 * WIDE) for block in (mine, other_core(mine))]
    near += [
        (block, 0, D + WIDE)
        for block in (before, behind, other_core(before), other_core(behind))
    ]
    sides = [(block, WIDE, 0) for block in (from_below, other_core(from_below))]
    sides += [(block, 0, D) for block in (from_above, other_core(from_above))]
    grad = product(near, core, weights)
    grad = product(sides, core, weights, grad, last=True)

    grad = reduced(grad) * coef
    grads = [grad]
    first, second = adam_moments(first, second, grad)
    param = adam_update(start, first, second, PRIOR + 1)

    grad = product(near + sides, core, gathered(param), last=True)
    grad = reduced(grad) * coef
    grads.append(grad)
    first, second = adam_moments(first, second, grad)
    param = adam_update(param, first, second, PRIOR + 2)

    leaving = jnp.stack([start - param, *grads]).astype(jnp.bfloat16)
    leaving = jnp.moveaxis(leaving.reshape(3, 8, 32, BLOCK), 1, 0)
    leaving = jnp.broadcast_to(leaving[None], (4, 8, 3, 32, BLOCK))
    arrived = exchange(leaving.reshape(32, 3, 32, BLOCK), ("h", "c", "yh", "yl", "x"))
    arrived = arrived.reshape(2, 2, 2, 2, 2, 3, 32, BLOCK)

    change = pick(pick(arrived[:, :, :, :, :, 0], (h + odd) % 2, 2), c, 1)
    change = jnp.sum(change.astype(jnp.float32), (0, 2))
    pseudo = jnp.moveaxis(change, 0, 1).reshape(32, WIDE) / 4
    new_mom = 0.9 * outer_mom + pseudo
    new_param = outer_param - 0.7 * (pseudo + 0.9 * new_mom)

    home = pick(pick(arrived[:, :, :, :, :, 1:], c, 4), h, 0)
    home = jnp.where(odd == 1, home[:, ::-1], home)
    home = home.transpose(3, 4, 1, 0, 2, 5).reshape(2, 32, 8 * BLOCK)
    first, second = first_mom[0], second_mom[0]
    for step in range(STEPS):
        first, second = adam_moments(first, second, home[step].astype(jnp.float32))
    return (new_param, new_mom, first[None], second[None])


def solution(mesh):
    fine = Mesh(
        mesh.devices.reshape(2, 2, 8, 2, 2, 2), ("h", "c", "z", "yh", "yl", "x")
    )
    group, fsdp = ("h", "c"), ("z", "yh", "yl", "x")
    in_specs = (
        P(group, fsdp, None),
        P(group, fsdp, None),
        P(group, None),
        P(fsdp, group),
        P(fsdp, group),
        P(group, fsdp, None),
        P(group, fsdp, None),
    )
    out_specs = (
        P(fsdp, group),
        P(fsdp, group),
        P(group, fsdp, None),
        P(group, fsdp, None),
    )
    return jax.shard_map(
        per_device, mesh=fine, in_specs=in_specs, out_specs=out_specs, check_vma=False
    )
```

```python
import functools

import jax
import jax.numpy as jnp
from jax import lax
from jax.experimental import pallas as pl
from jax.experimental.pallas import tpu as pltpu
from jax.sharding import Mesh
from jax.sharding import PartitionSpec as P

D = 2048
STEPS = 2
PRIOR = 1000
BLOCK = 128
TURN = [(0, 0), (1, 2), (2, 1), (3, 3)]
WIDE = 2 * BLOCK
PEERS = [[z * 4 + (colour + 2 * z) % 4 for z in range(8)] for colour in range(4)]


def adam_moments(first, second, grad):
    return 0.9 * first + 0.1 * grad, 0.95 * second + 0.05 * grad * grad


def adam_update(param, first, second, step):
    upd = first / (1.0 - 0.9**step) / (jnp.sqrt(second / (1.0 - 0.95**step)) + 1e-08)
    return param - 0.1 * (upd + 0.1 * param)


def shift(x, axis, by):
    size = lax.axis_size(axis)
    return lax.ppermute(x, axis, [(i, (i + by) % size) for i in range(size)])


def other_core(x):
    return shift(x, "c", 1)


def exchange(x, axes):
    return lax.all_to_all(x, axes, 0, 0, tiled=True)


def pick(x, index, axis):
    return lax.dynamic_index_in_dim(x, index, axis, keepdims=False)


def after(x, *earlier):
    return lax.optimization_barrier((x, *earlier))[0]


def turned(x):
    return lax.ppermute(x, ("c", "x"), TURN)


def up(x):
    return shift(x, ("yh", "yl"), 1)


def down(x):
    return shift(x, ("yh", "yl"), -1)


def place():
    z, y = lax.axis_index("z"), lax.axis_index("yh") * 2 + lax.axis_index("yl")
    odd = lax.rem(z, 2)
    return z, y, odd, lax.rem(y + 2 * odd, 4)


def prepare_kernel(lengths, tokens, targets, out):
    z, y, _, colour = place()
    length = lengths[0, (z * 4 + y) * 2 + lax.axis_index("x")]
    valid = lax.broadcasted_iota(jnp.int32, tokens.shape[1:], 0) < length
    inputs = tokens[0]
    out[:, WIDE : WIDE + D] = jnp.where(valid, inputs, jnp.zeros_like(inputs))
    for away, at in ((1, 0), (3, D + WIDE), (2, D + 2 * WIDE), (0, D + 3 * WIDE)):
        wanted = lax.rem(colour + away, 4)
        source = wanted // 2 * (2 * WIDE) + lax.rem(wanted, 2) * BLOCK
        for core in range(2):
            column = pl.multiple_of(source + core * WIDE, BLOCK)
            out[:, at + core * BLOCK : at + (core + 1) * BLOCK] = targets[
                0, :, pl.ds(column, BLOCK)
            ]


def prepare(lengths, tokens, targets):
    whole = pl.BlockSpec(memory_space=pltpu.VMEM)
    return pl.pallas_call(
        prepare_kernel,
        out_shape=jax.ShapeDtypeStruct((256, D + 4 * WIDE), jnp.bfloat16),
        in_specs=[pl.BlockSpec(memory_space=pltpu.SMEM), whole, whole],
        out_specs=whole,
        compiler_params=pltpu.CompilerParams(vmem_limit_bytes=16 * 2**20),
    )(lengths, tokens, targets)


def pack_kernel(lengths, param, first, second, weights, moments):
    _, _, odd, _ = place()
    count = lax.fori_loop(0, lengths.shape[1], lambda i, t: t + lengths[0, i], 0)
    count = (count // 128).astype(jnp.float32)
    for slot in range(16):
        core, yh, yl = slot // 8, slot // 4 % 2, slot // 2 % 2
        half = slice(yl * BLOCK, (yl + 1) * BLOCK)
        weights[slot] = param[:, half].astype(jnp.bfloat16)
        column = lax.rem(yh + odd, 2) * (2 * WIDE) + core * WIDE + yl * BLOCK
        columns = pl.ds(pl.multiple_of(column, BLOCK), BLOCK)
        moments[slot, 0:32] = first[0, :, columns].astype(jnp.bfloat16)
        moments[slot, 32:64] = second[0, :, columns].astype(jnp.bfloat16)
        moments[slot, 64:80] = jnp.full((16, BLOCK), count).astype(jnp.bfloat16)


def pack(lengths, param, first, second):
    whole = pl.BlockSpec(memory_space=pltpu.VMEM)
    return pl.pallas_call(
        pack_kernel,
        out_shape=[
            jax.ShapeDtypeStruct((16, 32, BLOCK), jnp.bfloat16),
            jax.ShapeDtypeStruct((16, 80, BLOCK), jnp.bfloat16),
        ],
        in_specs=[pl.BlockSpec(memory_space=pltpu.SMEM), whole, whole, whole],
        out_specs=[whole, whole],
        compiler_params=pltpu.CompilerParams(vmem_limit_bytes=16 * 2**20),
    )(lengths, param, first, second)


def finish_kernel(
    arrived, param, mom, first, second, new_param, new_mom, new_first, new_second
):
    _, _, odd, _ = place()
    h, c = lax.axis_index("h"), lax.axis_index("c")
    for yl in range(2):
        columns = slice(yl * BLOCK, (yl + 1) * BLOCK)
        total = jnp.zeros((32, BLOCK), jnp.float32)
        for group in range(4):
            yh = lax.rem(h + odd, 2)
            source = group // 2 * 16 + c * 8 + yh * 4 + yl * 2 + group % 2
            total += arrived[source, 0].astype(jnp.float32)
        pseudo = total / 4
        momentum = 0.9 * mom[:, columns] + pseudo
        new_mom[:, columns] = momentum
        new_param[:, columns] = param[:, columns] - 0.7 * (pseudo + 0.9 * momentum)
    for block in range(8):
        fh, core, fl = block // 4, block // 2 % 2, block % 2
        columns = slice(block * BLOCK, (block + 1) * BLOCK)
        source = h * 16 + core * 8 + lax.rem(fh + odd, 2) * 4 + fl * 2 + c
        moments = first[0, :, columns], second[0, :, columns]
        for step in range(STEPS):
            grad = arrived[source, 1 + step].astype(jnp.float32)
            moments = adam_moments(*moments, grad)
        new_first[0, :, columns], new_second[0, :, columns] = moments


def finish(*arrays):
    whole = pl.BlockSpec(memory_space=pltpu.VMEM)
    return pl.pallas_call(
        finish_kernel,
        out_shape=[jax.ShapeDtypeStruct(a.shape, a.dtype) for a in arrays[1:]],
        in_specs=[whole] * 5,
        out_specs=[whole] * 4,
        compiler_params=pltpu.CompilerParams(vmem_limit_bytes=16 * 2**20),
    )(*arrays)


def product_kernel(layout, last, core, weights, *refs):
    count = len(layout)
    blocks, refs = refs[:count], refs[count:]
    earlier, out, held, goals, total, sems = refs if len(refs) == 6 else (None, *refs)
    copies, row = [], 0
    for at, (rows, inputs_at, goals_at) in enumerate(layout):
        half = pl.multiple_of(goals_at + core[0] * BLOCK, BLOCK)
        sources = blocks[at].at[:, pl.ds(inputs_at, D)], blocks[at].at[:, pl.ds(half, BLOCK)]
        here = pl.ds(row, rows)
        for kind, (source, target) in enumerate(zip(sources, (held, goals))):
            copy = pltpu.make_async_copy(source, target.at[here], sems.at[kind, at])
            copy.start()
            copies.append(copy)
        row += rows
    if earlier is not None:
        total[...] = earlier[...]
    row = at = 0
    while at < count:
        size = 0
        while size < 512:
            copies[2 * at].wait()
            copies[2 * at + 1].wait()
            size += layout[at][0]
            at += 1
        inputs = held[row : row + size]
        goal = goals[row : row + size].astype(jnp.float32)
        outputs = jnp.dot(inputs, weights[...], preferred_element_type=jnp.float32)
        resid = (outputs * D ** (-0.5) - goal).astype(jnp.bfloat16)
        grad = lax.dot_general(
            resid, inputs, (((0,), (0,)), ((), ())), preferred_element_type=jnp.float32
        )
        if row == 0 and earlier is None:
            total[...] = grad
        else:
            total[...] += grad
        row += size
    if last:
        for z in range(8):
            out[z] = total[:, z * 256 : (z + 1) * 256].T.astype(jnp.bfloat16)
    else:
        out[...] = total[...]


def product(parts, core, weights, earlier=None, last=False):
    blocks = [block for block, _, _ in parts]
    layout = [(block.shape[0], *places) for block, *places in parts]
    rows = sum(block.shape[0] for block in blocks)
    whole = pl.BlockSpec(memory_space=pltpu.VMEM)
    args = [core, weights, *blocks]
    specs = [pl.BlockSpec(memory_space=pltpu.SMEM), whole]
    specs += [pl.BlockSpec(memory_space=pl.ANY)] * len(blocks)
    if earlier is not None:
        args.append(earlier)
        specs.append(whole)
    shape = ((8, 256, BLOCK), jnp.bfloat16) if last else ((BLOCK, D), jnp.float32)
    return pl.pallas_call(
        functools.partial(product_kernel, layout, last),
        out_shape=jax.ShapeDtypeStruct(*shape),
        in_specs=specs,
        out_specs=whole,
        scratch_shapes=[
            pltpu.VMEM((rows, D), jnp.bfloat16),
            pltpu.VMEM((rows, BLOCK), jnp.bfloat16),
            pltpu.VMEM((BLOCK, D), jnp.float32),
            pltpu.SemaphoreType.DMA((2, len(blocks))),
        ],
        compiler_params=pltpu.CompilerParams(vmem_limit_bytes=40 * 2**20),
        cost_estimate=pl.CostEstimate(
            flops=8 * rows * D * BLOCK, bytes_accessed=2 * rows * D, transcendentals=0
        ),
    )(*args)


def among_peers(x):
    axes = ("z", "yh", "yl")
    return lax.all_to_all(x, axes, 0, 0, axis_index_groups=PEERS, tiled=True)


def gathered(param):
    weights = jnp.broadcast_to(param.astype(jnp.bfloat16)[None], (8, 256, BLOCK))
    return among_peers(weights).reshape(D, BLOCK)


def reduced(grad):
    return jnp.sum(among_peers(grad).astype(jnp.float32), 0)


def per_device(tokens, targets, lengths, outer_param, outer_mom, first_mom, second_mom):
    c, x = lax.axis_index("c"), lax.axis_index("x")
    _, _, odd, colour = place()
    core = c.reshape(1).astype(jnp.int32)

    mine = turned(prepare(lengths, tokens, targets))
    from_below = up(mine[:, : D + WIDE])
    from_above = down(mine[:, WIDE : D + 2 * WIDE])

    start, moments = pack(lengths, outer_param, first_mom, second_mom)
    start = exchange(start, ("h", "yh", "yl", "x"))
    start = start.reshape(2, 256, BLOCK)
    here = pick(start, colour // 2, 0)
    there = pick(start, 1 - colour // 2, 0)
    weights = jnp.where(
        (jnp.arange(8) % 2 == odd)[:, None, None], here[None], there[None]
    )
    weights = exchange(weights, "z").reshape(D, BLOCK)
    start = here.astype(jnp.float32)
    mine = after(mine, weights)
    half = mine.shape[0] // 2
    before = shift(mine[:half, WIDE : D + 3 * WIDE], "z", 1)
    behind = shift(mine[half:, WIDE : D + 3 * WIDE], "z", -1)

    moments = exchange(after(moments, weights), ("c", "yh", "yl", "x"))
    moments = pick(moments.reshape(2, 8, 80, BLOCK), x, 0)
    from_below, from_above, moments = lax.optimization_barrier(
        (from_below, from_above, moments)
    )
    near = [(block, WIDE, D + 3 * WIDE) for block in (mine, other_core(mine))]
    near += [
        (block, 0, D + WIDE)
        for block in (before, behind, other_core(before), other_core(behind))
    ]
    sides = [(block, WIDE, 0) for block in (from_below, other_core(from_below))]
    sides += [(block, 0, D) for block in (from_above, other_core(from_above))]
    grad = product(near, core, weights)
    grad = product(sides, core, weights, grad, last=True)

    first = moments[:, :32].reshape(256, BLOCK).astype(jnp.float32)
    second = moments[:, 32:64].reshape(256, BLOCK).astype(jnp.float32)
    coef = D ** (-0.5) / (128.0 * moments[0, 64, 0].astype(jnp.float32))
    grad = reduced(grad) * coef
    grads = [grad]
    first, second = adam_moments(first, second, grad)
    param = adam_update(start, first, second, PRIOR + 1)

    grad = product(near + sides, core, gathered(param), last=True)
    grad = reduced(grad) * coef
    grads.append(grad)
    first, second = adam_moments(first, second, grad)
    param = adam_update(param, first, second, PRIOR + 2)

    leaving = jnp.stack([start - param, *grads]).astype(jnp.bfloat16)
    leaving = jnp.moveaxis(leaving.reshape(3, 8, 32, BLOCK), 1, 0)
    leaving = jnp.broadcast_to(leaving[None], (4, 8, 3, 32, BLOCK))
    arrived = exchange(leaving.reshape(32, 3, 32, BLOCK), ("h", "c", "yh", "yl", "x"))
    return tuple(finish(arrived, outer_param, outer_mom, first_mom, second_mom))


def solution(mesh):
    fine = Mesh(
        mesh.devices.reshape(2, 2, 8, 2, 2, 2), ("h", "c", "z", "yh", "yl", "x")
    )
    group, fsdp = ("h", "c"), ("z", "yh", "yl", "x")
    in_specs = (
        P(group, fsdp, None),
        P(group, fsdp, None),
        P(group, None),
        P(fsdp, group),
        P(fsdp, group),
        P(group, fsdp, None),
        P(group, fsdp, None),
    )
    out_specs = (
        P(fsdp, group),
        P(fsdp, group),
        P(group, fsdp, None),
        P(group, fsdp, None),
    )
    return jax.shard_map(
        per_device, mesh=fine, in_specs=in_specs, out_specs=out_specs, check_vma=False
    )
```

```python
import functools

import jax
import jax.numpy as jnp
from jax import lax
from jax.experimental import pallas as pl
from jax.experimental.pallas import tpu as pltpu
from jax.sharding import Mesh
from jax.sharding import PartitionSpec as P

D = 2048
STEPS = 2
PRIOR = 1000
BLOCK = 128
TURN = [(0, 0), (1, 2), (2, 1), (3, 3)]
WIDE = 2 * BLOCK
PEERS = [[z * 4 + (colour + 2 * z) % 4 for z in range(8)] for colour in range(4)]


def adam_moments(first, second, grad):
    return 0.9 * first + 0.1 * grad, 0.95 * second + 0.05 * grad * grad


def adam_update(param, first, second, step):
    upd = first / (1.0 - 0.9**step) / (jnp.sqrt(second / (1.0 - 0.95**step)) + 1e-08)
    return param - 0.1 * (upd + 0.1 * param)


def shift(x, axis, by):
    size = lax.axis_size(axis)
    return lax.ppermute(x, axis, [(i, (i + by) % size) for i in range(size)])


def other_core(x):
    return shift(x, "c", 1)


def exchange(x, axes):
    return lax.all_to_all(x, axes, 0, 0, tiled=True)


def pick(x, index, axis):
    return lax.dynamic_index_in_dim(x, index, axis, keepdims=False)


def together(*arrays):
    return lax.optimization_barrier(arrays)


def turned(x):
    return lax.ppermute(x, ("c", "x"), TURN)


def up(x):
    return shift(x, ("yh", "yl"), 1)


def down(x):
    return shift(x, ("yh", "yl"), -1)


def place():
    z, y = lax.axis_index("z"), lax.axis_index("yh") * 2 + lax.axis_index("yl")
    odd = lax.rem(z, 2)
    return z, y, odd, lax.rem(y + 2 * odd, 4)


def prepare_kernel(lengths, tokens, targets, out, inputs, goals, sems):
    copies = [
        pltpu.make_async_copy(tokens.at[0], inputs, sems.at[0]),
        pltpu.make_async_copy(targets.at[0], goals, sems.at[1]),
    ]
    for copy in copies:
        copy.start()
    z, y, _, colour = place()
    length = lengths[0, (z * 4 + y) * 2 + lax.axis_index("x")]
    valid = lax.broadcasted_iota(jnp.int32, inputs.shape, 0) < length
    copies[0].wait()
    out[:, WIDE : WIDE + D] = jnp.where(valid, inputs[...], jnp.zeros_like(inputs))
    copies[1].wait()
    for away, at in ((1, 0), (3, D + WIDE), (2, D + 2 * WIDE), (0, D + 3 * WIDE)):
        wanted = lax.rem(colour + away, 4)
        source = wanted // 2 * (2 * WIDE) + lax.rem(wanted, 2) * BLOCK
        for core in range(2):
            column = pl.multiple_of(source + core * WIDE, BLOCK)
            out[:, at + core * BLOCK : at + (core + 1) * BLOCK] = goals[
                :, pl.ds(column, BLOCK)
            ]


def prepare(lengths, tokens, targets):
    rows = tokens.shape[1]
    return pl.pallas_call(
        prepare_kernel,
        out_shape=jax.ShapeDtypeStruct((rows, D + 4 * WIDE), jnp.bfloat16),
        in_specs=[pl.BlockSpec(memory_space=pltpu.SMEM)]
        + [pl.BlockSpec(memory_space=pl.ANY)] * 2,
        out_specs=pl.BlockSpec(memory_space=pltpu.VMEM),
        scratch_shapes=[
            pltpu.VMEM((rows, D), jnp.bfloat16),
            pltpu.VMEM((rows, 4 * WIDE), jnp.bfloat16),
            pltpu.SemaphoreType.DMA((2,)),
        ],
        compiler_params=pltpu.CompilerParams(vmem_limit_bytes=60 * 2**20),
    )(lengths, tokens, targets)


def pack_kernel(lengths, param, first, second, weights, moments):
    _, _, odd, _ = place()
    count = lax.fori_loop(0, lengths.shape[1], lambda i, t: t + lengths[0, i], 0)
    count = (count // 128).astype(jnp.float32)
    for slot in range(16):
        core, yh, yl = slot // 8, slot // 4 % 2, slot // 2 % 2
        half = slice(yl * BLOCK, (yl + 1) * BLOCK)
        weights[slot] = param[:, half].astype(jnp.bfloat16)
        column = lax.rem(yh + odd, 2) * (2 * WIDE) + core * WIDE + yl * BLOCK
        columns = pl.ds(pl.multiple_of(column, BLOCK), BLOCK)
        moments[slot, 0:32] = first[0, :, columns].astype(jnp.bfloat16)
        moments[slot, 32:64] = second[0, :, columns].astype(jnp.bfloat16)
        moments[slot, 64:80] = jnp.full((16, BLOCK), count).astype(jnp.bfloat16)


def pack(lengths, param, first, second):
    whole = pl.BlockSpec(memory_space=pltpu.VMEM)
    return pl.pallas_call(
        pack_kernel,
        out_shape=[
            jax.ShapeDtypeStruct((16, 32, BLOCK), jnp.bfloat16),
            jax.ShapeDtypeStruct((16, 80, BLOCK), jnp.bfloat16),
        ],
        in_specs=[pl.BlockSpec(memory_space=pltpu.SMEM), whole, whole, whole],
        out_specs=[whole, whole],
        compiler_params=pltpu.CompilerParams(vmem_limit_bytes=16 * 2**20),
    )(lengths, param, first, second)


def finish_kernel(
    arrived, param, mom, first, second, new_param, new_mom, new_first, new_second
):
    _, _, odd, _ = place()
    h, c = lax.axis_index("h"), lax.axis_index("c")
    for yl in range(2):
        columns = slice(yl * BLOCK, (yl + 1) * BLOCK)
        total = jnp.zeros((32, BLOCK), jnp.float32)
        for group in range(4):
            yh = lax.rem(h + odd, 2)
            source = group // 2 * 16 + c * 8 + yh * 4 + yl * 2 + group % 2
            total += arrived[source, 0].astype(jnp.float32)
        pseudo = total / 4
        momentum = 0.9 * mom[:, columns] + pseudo
        new_mom[:, columns] = momentum
        new_param[:, columns] = param[:, columns] - 0.7 * (pseudo + 0.9 * momentum)
    for block in range(8):
        fh, core, fl = block // 4, block // 2 % 2, block % 2
        columns = slice(block * BLOCK, (block + 1) * BLOCK)
        source = h * 16 + core * 8 + lax.rem(fh + odd, 2) * 4 + fl * 2 + c
        moments = first[0, :, columns], second[0, :, columns]
        for step in range(STEPS):
            grad = arrived[source, 1 + step].astype(jnp.float32)
            moments = adam_moments(*moments, grad)
        new_first[0, :, columns], new_second[0, :, columns] = moments


def finish(*arrays):
    whole = pl.BlockSpec(memory_space=pltpu.VMEM)
    return pl.pallas_call(
        finish_kernel,
        out_shape=[jax.ShapeDtypeStruct(a.shape, a.dtype) for a in arrays[1:]],
        in_specs=[whole] * 5,
        out_specs=[whole] * 4,
        compiler_params=pltpu.CompilerParams(vmem_limit_bytes=16 * 2**20),
    )(*arrays)


def product_kernel(layout, last, core, weights, *refs):
    count = len(layout)
    blocks, refs = refs[:count], refs[count:]
    earlier, out, held, goals, total, sems = refs if len(refs) == 6 else (None, *refs)
    copies, row = [], 0
    for at, (rows, inputs_at, goals_at) in enumerate(layout):
        half = pl.multiple_of(goals_at + core[0] * BLOCK, BLOCK)
        sources = blocks[at].at[:, pl.ds(inputs_at, D)], blocks[at].at[:, pl.ds(half, BLOCK)]
        here = pl.ds(row, rows)
        for kind, (source, target) in enumerate(zip(sources, (held, goals))):
            copy = pltpu.make_async_copy(source, target.at[here], sems.at[kind, at])
            copy.start()
            copies.append(copy)
        row += rows
    if earlier is not None:
        total[...] = earlier[...]
    row = at = 0
    while at < count:
        size = 0
        while size < 512:
            copies[2 * at].wait()
            copies[2 * at + 1].wait()
            size += layout[at][0]
            at += 1
        inputs = held[row : row + size]
        goal = goals[row : row + size].astype(jnp.float32)
        outputs = jnp.dot(inputs, weights[...], preferred_element_type=jnp.float32)
        resid = (outputs * D ** (-0.5) - goal).astype(jnp.bfloat16)
        grad = lax.dot_general(
            resid, inputs, (((0,), (0,)), ((), ())), preferred_element_type=jnp.float32
        )
        if row == 0 and earlier is None:
            total[...] = grad
        else:
            total[...] += grad
        row += size
    if last:
        for z in range(8):
            out[z] = total[:, z * 256 : (z + 1) * 256].T.astype(jnp.bfloat16)
    else:
        out[...] = total[...]


def product(parts, core, weights, earlier=None, last=False):
    blocks = [block for block, _, _ in parts]
    layout = [(block.shape[0], *places) for block, *places in parts]
    rows = sum(block.shape[0] for block in blocks)
    whole = pl.BlockSpec(memory_space=pltpu.VMEM)
    args = [core, weights, *blocks]
    specs = [pl.BlockSpec(memory_space=pltpu.SMEM), whole]
    specs += [pl.BlockSpec(memory_space=pl.ANY)] * len(blocks)
    if earlier is not None:
        args.append(earlier)
        specs.append(whole)
    shape = ((8, 256, BLOCK), jnp.bfloat16) if last else ((BLOCK, D), jnp.float32)
    return pl.pallas_call(
        functools.partial(product_kernel, layout, last),
        out_shape=jax.ShapeDtypeStruct(*shape),
        in_specs=specs,
        out_specs=whole,
        scratch_shapes=[
            pltpu.VMEM((rows, D), jnp.bfloat16),
            pltpu.VMEM((rows, BLOCK), jnp.bfloat16),
            pltpu.VMEM((BLOCK, D), jnp.float32),
            pltpu.SemaphoreType.DMA((2, len(blocks))),
        ],
        compiler_params=pltpu.CompilerParams(vmem_limit_bytes=40 * 2**20),
        cost_estimate=pl.CostEstimate(
            flops=8 * rows * D * BLOCK, bytes_accessed=2 * rows * D, transcendentals=0
        ),
    )(*args)


def among_peers(x):
    axes = ("z", "yh", "yl")
    return lax.all_to_all(x, axes, 0, 0, axis_index_groups=PEERS, tiled=True)


def gathered(param):
    weights = jnp.broadcast_to(param.astype(jnp.bfloat16)[None], (8, 256, BLOCK))
    return among_peers(weights).reshape(D, BLOCK)


def reduced(grad):
    return jnp.sum(among_peers(grad).astype(jnp.float32), 0)


def per_device(tokens, targets, lengths, outer_param, outer_mom, first_mom, second_mom):
    c, x = lax.axis_index("c"), lax.axis_index("x")
    _, _, odd, colour = place()
    core = c.reshape(1).astype(jnp.int32)

    mine = turned(prepare(lengths, tokens, targets))
    start, moments = pack(lengths, outer_param, first_mom, second_mom)
    start = exchange(start, ("h", "yh", "yl", "x"))
    mine, start = together(mine, start)
    theirs = other_core(mine)

    below, above = up(mine[:, : D + WIDE]), down(mine[:, WIDE : D + 2 * WIDE])
    half = mine.shape[0] // 2
    plane = jnp.concatenate(
        [mine[:, WIDE : WIDE + D], mine[:, D + 2 * WIDE : D + 3 * WIDE]], 1
    )
    before, behind = shift(plane[:half], "z", 1), shift(plane[half:], "z", -1)

    start = start.reshape(2, 256, BLOCK)
    here = pick(start, colour // 2, 0)
    there = pick(start, 1 - colour // 2, 0)
    weights = jnp.where(
        (jnp.arange(8) % 2 == odd)[:, None, None], here[None], there[None]
    )
    weights = exchange(weights, "z").reshape(D, BLOCK)
    start = here.astype(jnp.float32)

    moments, weights = together(moments, weights)
    moments = exchange(moments, ("c", "yh", "yl", "x"))
    moments = pick(moments.reshape(2, 8, 80, BLOCK), x, 0)

    weights, above = together(weights, above)
    near = [(block, WIDE, D + 3 * WIDE) for block in (mine, theirs)]
    near += [
        (block, 0, D)
        for block in (before, behind, other_core(before), other_core(behind))
    ]
    sides = [(block, WIDE, 0) for block in (below, other_core(below))]
    sides += [(block, 0, D) for block in (above, other_core(above))]
    grad = product(near, core, weights)
    grad = product(sides, core, weights, grad, last=True)

    first = moments[:, :32].reshape(256, BLOCK).astype(jnp.float32)
    second = moments[:, 32:64].reshape(256, BLOCK).astype(jnp.float32)
    coef = D ** (-0.5) / (128.0 * moments[0, 64, 0].astype(jnp.float32))
    grad = reduced(grad) * coef
    grads = [grad]
    first, second = adam_moments(first, second, grad)
    param = adam_update(start, first, second, PRIOR + 1)

    grad = product(near + sides, core, gathered(param), last=True)
    grad = reduced(grad) * coef
    grads.append(grad)
    first, second = adam_moments(first, second, grad)
    param = adam_update(param, first, second, PRIOR + 2)

    leaving = jnp.stack([start - param, *grads]).astype(jnp.bfloat16)
    leaving = jnp.moveaxis(leaving.reshape(3, 8, 32, BLOCK), 1, 0)
    leaving = jnp.broadcast_to(leaving[None], (4, 8, 3, 32, BLOCK))
    arrived = exchange(leaving.reshape(32, 3, 32, BLOCK), ("h", "c", "yh", "yl", "x"))
    return tuple(finish(arrived, outer_param, outer_mom, first_mom, second_mom))


def solution(mesh):
    fine = Mesh(
        mesh.devices.reshape(2, 2, 8, 2, 2, 2), ("h", "c", "z", "yh", "yl", "x")
    )
    group, fsdp = ("h", "c"), ("z", "yh", "yl", "x")
    in_specs = (
        P(group, fsdp, None),
        P(group, fsdp, None),
        P(group, None),
        P(fsdp, group),
        P(fsdp, group),
        P(group, fsdp, None),
        P(group, fsdp, None),
    )
    out_specs = (
        P(fsdp, group),
        P(fsdp, group),
        P(group, fsdp, None),
        P(group, fsdp, None),
    )
    return jax.shard_map(
        per_device, mesh=fine, in_specs=in_specs, out_specs=out_specs, check_vma=False
    )
```

```python
import functools

import jax
import jax.numpy as jnp
from jax import lax
from jax.experimental import pallas as pl
from jax.experimental.pallas import tpu as pltpu
from jax.sharding import Mesh
from jax.sharding import PartitionSpec as P

D = 2048
STEPS = 2
PRIOR = 1000
BLOCK = 128
TURN = [(0, 0), (1, 2), (2, 1), (3, 3)]
WIDE = 2 * BLOCK
PEERS = [[z * 4 + (colour + 2 * z) % 4 for z in range(8)] for colour in range(4)]


def adam_moments(first, second, grad):
    return 0.9 * first + 0.1 * grad, 0.95 * second + 0.05 * grad * grad


def adam_update(param, first, second, step):
    upd = first / (1.0 - 0.9**step) / (jnp.sqrt(second / (1.0 - 0.95**step)) + 1e-08)
    return param - 0.1 * (upd + 0.1 * param)


def shift(x, axis, by):
    size = lax.axis_size(axis)
    return lax.ppermute(x, axis, [(i, (i + by) % size) for i in range(size)])


def other_core(x):
    return shift(x, "c", 1)


def exchange(x, axes):
    return lax.all_to_all(x, axes, 0, 0, tiled=True)


def pick(x, index, axis):
    return lax.dynamic_index_in_dim(x, index, axis, keepdims=False)


def together(*arrays):
    return lax.optimization_barrier(arrays)


def turned(x):
    return lax.ppermute(x, ("c", "x"), TURN)


def up(x):
    return shift(x, ("yh", "yl"), 1)


def down(x):
    return shift(x, ("yh", "yl"), -1)


def place():
    z, y = lax.axis_index("z"), lax.axis_index("yh") * 2 + lax.axis_index("yl")
    odd = lax.rem(z, 2)
    return z, y, odd, lax.rem(y + 2 * odd, 4)


def prepare_kernel(lengths, tokens, targets, out, inputs, goals, sems):
    copies = [
        pltpu.make_async_copy(tokens.at[0], inputs, sems.at[0]),
        pltpu.make_async_copy(targets.at[0], goals, sems.at[1]),
    ]
    for copy in copies:
        copy.start()
    z, y, _, colour = place()
    length = lengths[0, (z * 4 + y) * 2 + lax.axis_index("x")]
    valid = lax.broadcasted_iota(jnp.int32, inputs.shape, 0) < length
    copies[0].wait()
    out[:, WIDE : WIDE + D] = jnp.where(valid, inputs[...], jnp.zeros_like(inputs))
    copies[1].wait()
    for away, at in ((1, 0), (3, D + WIDE), (2, D + 2 * WIDE), (0, D + 3 * WIDE)):
        wanted = lax.rem(colour + away, 4)
        source = wanted // 2 * (2 * WIDE) + lax.rem(wanted, 2) * BLOCK
        for core in range(2):
            column = pl.multiple_of(source + core * WIDE, BLOCK)
            out[:, at + core * BLOCK : at + (core + 1) * BLOCK] = goals[
                :, pl.ds(column, BLOCK)
            ]


def prepare(lengths, tokens, targets):
    rows = tokens.shape[1]
    return pl.pallas_call(
        prepare_kernel,
        out_shape=jax.ShapeDtypeStruct((rows, D + 4 * WIDE), jnp.bfloat16),
        in_specs=[pl.BlockSpec(memory_space=pltpu.SMEM)]
        + [pl.BlockSpec(memory_space=pl.ANY)] * 2,
        out_specs=pl.BlockSpec(memory_space=pltpu.VMEM),
        scratch_shapes=[
            pltpu.VMEM((rows, D), jnp.bfloat16),
            pltpu.VMEM((rows, 4 * WIDE), jnp.bfloat16),
            pltpu.SemaphoreType.DMA((2,)),
        ],
        compiler_params=pltpu.CompilerParams(vmem_limit_bytes=60 * 2**20),
    )(lengths, tokens, targets)


def pack_kernel(lengths, param, first, second, weights, moments):
    _, _, odd, _ = place()
    count = lax.fori_loop(0, lengths.shape[1], lambda i, t: t + lengths[0, i], 0)
    count = (count // 128).astype(jnp.float32)
    for slot in range(16):
        core, yh, yl = slot // 8, slot // 4 % 2, slot // 2 % 2
        half = slice(yl * BLOCK, (yl + 1) * BLOCK)
        weights[slot] = param[:, half].astype(jnp.bfloat16)
        column = lax.rem(yh + odd, 2) * (2 * WIDE) + core * WIDE + yl * BLOCK
        columns = pl.ds(pl.multiple_of(column, BLOCK), BLOCK)
        moments[slot, 0:32] = first[0, :, columns].astype(jnp.bfloat16)
        moments[slot, 32:64] = second[0, :, columns].astype(jnp.bfloat16)
        moments[slot, 64:80] = jnp.full((16, BLOCK), count).astype(jnp.bfloat16)


def pack(lengths, param, first, second):
    whole = pl.BlockSpec(memory_space=pltpu.VMEM)
    return pl.pallas_call(
        pack_kernel,
        out_shape=[
            jax.ShapeDtypeStruct((16, 32, BLOCK), jnp.bfloat16),
            jax.ShapeDtypeStruct((16, 80, BLOCK), jnp.bfloat16),
        ],
        in_specs=[pl.BlockSpec(memory_space=pltpu.SMEM), whole, whole, whole],
        out_specs=[whole, whole],
        compiler_params=pltpu.CompilerParams(vmem_limit_bytes=16 * 2**20),
    )(lengths, param, first, second)


def finish_kernel(
    arrived, param, mom, first, second, new_param, new_mom, new_first, new_second
):
    _, _, odd, _ = place()
    h, c = lax.axis_index("h"), lax.axis_index("c")
    for yl in range(2):
        columns = slice(yl * BLOCK, (yl + 1) * BLOCK)
        total = jnp.zeros((32, BLOCK), jnp.float32)
        for group in range(4):
            yh = lax.rem(h + odd, 2)
            source = group // 2 * 16 + c * 8 + yh * 4 + yl * 2 + group % 2
            total += arrived[source, 0].astype(jnp.float32)
        pseudo = total / 4
        momentum = 0.9 * mom[:, columns] + pseudo
        new_mom[:, columns] = momentum
        new_param[:, columns] = param[:, columns] - 0.7 * (pseudo + 0.9 * momentum)
    for block in range(8):
        fh, core, fl = block // 4, block // 2 % 2, block % 2
        columns = slice(block * BLOCK, (block + 1) * BLOCK)
        source = h * 16 + core * 8 + lax.rem(fh + odd, 2) * 4 + fl * 2 + c
        moments = first[0, :, columns], second[0, :, columns]
        for step in range(STEPS):
            grad = arrived[source, 1 + step].astype(jnp.float32)
            moments = adam_moments(*moments, grad)
        new_first[0, :, columns], new_second[0, :, columns] = moments


def finish(*arrays):
    whole = pl.BlockSpec(memory_space=pltpu.VMEM)
    return pl.pallas_call(
        finish_kernel,
        out_shape=[jax.ShapeDtypeStruct(a.shape, a.dtype) for a in arrays[1:]],
        in_specs=[whole] * 5,
        out_specs=[whole] * 4,
        compiler_params=pltpu.CompilerParams(vmem_limit_bytes=16 * 2**20),
    )(*arrays)


def product_kernel(layout, last, core, weights, *refs):
    count = len(layout)
    blocks, refs = refs[:count], refs[count:]
    earlier, out, held, goals, total, sems = refs if len(refs) == 6 else (None, *refs)
    copies, row = [], 0
    for at, (rows, inputs_at, goals_at) in enumerate(layout):
        half = pl.multiple_of(goals_at + core[0] * BLOCK, BLOCK)
        sources = blocks[at].at[:, pl.ds(inputs_at, D)], blocks[at].at[:, pl.ds(half, BLOCK)]
        here = pl.ds(row, rows)
        for kind, (source, target) in enumerate(zip(sources, (held, goals))):
            copy = pltpu.make_async_copy(source, target.at[here], sems.at[kind, at])
            copy.start()
            copies.append(copy)
        row += rows
    if earlier is not None:
        total[...] = earlier[...]
    row = at = 0
    while at < count:
        size = 0
        while size < 512:
            copies[2 * at].wait()
            copies[2 * at + 1].wait()
            size += layout[at][0]
            at += 1
        inputs = held[row : row + size]
        goal = goals[row : row + size].astype(jnp.float32)
        outputs = jnp.dot(inputs, weights[...], preferred_element_type=jnp.float32)
        resid = (outputs * D ** (-0.5) - goal).astype(jnp.bfloat16)
        grad = lax.dot_general(
            resid, inputs, (((0,), (0,)), ((), ())), preferred_element_type=jnp.float32
        )
        if row == 0 and earlier is None:
            total[...] = grad
        else:
            total[...] += grad
        row += size
    if last:
        for z in range(8):
            out[z] = total[:, z * 256 : (z + 1) * 256].T.astype(jnp.bfloat16)
    else:
        out[...] = total[...]


def product(parts, core, weights, earlier=None, last=False):
    blocks = [block for block, _, _ in parts]
    layout = [(block.shape[0], *places) for block, *places in parts]
    rows = sum(block.shape[0] for block in blocks)
    whole = pl.BlockSpec(memory_space=pltpu.VMEM)
    args = [core, weights, *blocks]
    specs = [pl.BlockSpec(memory_space=pltpu.SMEM), whole]
    specs += [pl.BlockSpec(memory_space=pl.ANY)] * len(blocks)
    if earlier is not None:
        args.append(earlier)
        specs.append(whole)
    shape = ((8, 256, BLOCK), jnp.bfloat16) if last else ((BLOCK, D), jnp.float32)
    return pl.pallas_call(
        functools.partial(product_kernel, layout, last),
        out_shape=jax.ShapeDtypeStruct(*shape),
        in_specs=specs,
        out_specs=whole,
        scratch_shapes=[
            pltpu.VMEM((rows, D), jnp.bfloat16),
            pltpu.VMEM((rows, BLOCK), jnp.bfloat16),
            pltpu.VMEM((BLOCK, D), jnp.float32),
            pltpu.SemaphoreType.DMA((2, len(blocks))),
        ],
        compiler_params=pltpu.CompilerParams(vmem_limit_bytes=40 * 2**20),
        cost_estimate=pl.CostEstimate(
            flops=8 * rows * D * BLOCK, bytes_accessed=2 * rows * D, transcendentals=0
        ),
    )(*args)


def among_peers(x):
    axes = ("z", "yh", "yl")
    return lax.all_to_all(x, axes, 0, 0, axis_index_groups=PEERS, tiled=True)


def gathered(param):
    weights = jnp.broadcast_to(param.astype(jnp.bfloat16)[None], (8, 256, BLOCK))
    return among_peers(weights).reshape(D, BLOCK)


def reduced(grad):
    return jnp.sum(among_peers(grad).astype(jnp.float32), 0)


def per_device(tokens, targets, lengths, outer_param, outer_mom, first_mom, second_mom):
    c, x = lax.axis_index("c"), lax.axis_index("x")
    _, _, odd, colour = place()
    core = c.reshape(1).astype(jnp.int32)

    start, moments = pack(lengths, outer_param, first_mom, second_mom)
    start = exchange(start, ("h", "yh", "yl", "x"))
    mine, start = together(prepare(lengths, tokens, targets), start)
    mine = turned(mine)
    theirs = other_core(mine)

    below, above = up(mine[:, : D + WIDE]), down(mine[:, WIDE : D + 2 * WIDE])
    half = mine.shape[0] // 2
    plane = jnp.concatenate(
        [mine[:, WIDE : WIDE + D], mine[:, D + 2 * WIDE : D + 3 * WIDE]], 1
    )

    start = start.reshape(2, 256, BLOCK)
    here = pick(start, colour // 2, 0)
    there = pick(start, 1 - colour // 2, 0)
    weights = jnp.where(
        (jnp.arange(8) % 2 == odd)[:, None, None], here[None], there[None]
    )
    weights = exchange(weights, "z").reshape(D, BLOCK)
    start = here.astype(jnp.float32)
    plane, weights = together(plane, weights)
    before, behind = shift(plane[:half], "z", 1), shift(plane[half:], "z", -1)

    moments, weights = together(moments, weights)
    moments = exchange(moments, ("c", "yh", "yl", "x"))
    moments = pick(moments.reshape(2, 8, 80, BLOCK), x, 0)

    near = [(block, WIDE, D + 3 * WIDE) for block in (mine, theirs)]
    near += [
        (block, 0, D)
        for block in (before, behind, other_core(before), other_core(behind))
    ]
    moments, below, above = together(moments, below, above)
    sides = [(block, WIDE, 0) for block in (below, other_core(below))]
    sides += [(block, 0, D) for block in (above, other_core(above))]
    grad = product(near, core, weights)
    grad = product(sides, core, weights, grad, last=True)

    first = moments[:, :32].reshape(256, BLOCK).astype(jnp.float32)
    second = moments[:, 32:64].reshape(256, BLOCK).astype(jnp.float32)
    coef = D ** (-0.5) / (128.0 * moments[0, 64, 0].astype(jnp.float32))
    grad = reduced(grad) * coef
    grads = [grad]
    first, second = adam_moments(first, second, grad)
    param = adam_update(start, first, second, PRIOR + 1)

    grad = product(near + sides, core, gathered(param), last=True)
    grad = reduced(grad) * coef
    grads.append(grad)
    first, second = adam_moments(first, second, grad)
    param = adam_update(param, first, second, PRIOR + 2)

    leaving = jnp.stack([start - param, *grads]).astype(jnp.bfloat16)
    leaving = jnp.moveaxis(leaving.reshape(3, 8, 32, BLOCK), 1, 0)
    leaving = jnp.broadcast_to(leaving[None], (4, 8, 3, 32, BLOCK))
    arrived = exchange(leaving.reshape(32, 3, 32, BLOCK), ("h", "c", "yh", "yl", "x"))
    return tuple(finish(arrived, outer_param, outer_mom, first_mom, second_mom))


def solution(mesh):
    fine = Mesh(
        mesh.devices.reshape(2, 2, 8, 2, 2, 2), ("h", "c", "z", "yh", "yl", "x")
    )
    group, fsdp = ("h", "c"), ("z", "yh", "yl", "x")
    in_specs = (
        P(group, fsdp, None),
        P(group, fsdp, None),
        P(group, None),
        P(fsdp, group),
        P(fsdp, group),
        P(group, fsdp, None),
        P(group, fsdp, None),
    )
    out_specs = (
        P(fsdp, group),
        P(fsdp, group),
        P(group, fsdp, None),
        P(group, fsdp, None),
    )
    return jax.shard_map(
        per_device, mesh=fine, in_specs=in_specs, out_specs=out_specs, check_vma=False
    )
```

```python
import functools

import jax
import jax.numpy as jnp
from jax import lax
from jax.experimental import pallas as pl
from jax.experimental.pallas import tpu as pltpu
from jax.sharding import Mesh
from jax.sharding import PartitionSpec as P

D = 2048
STEPS = 2
PRIOR = 1000
BLOCK = 128
TURN = [(0, 0), (1, 2), (2, 1), (3, 3)]
WIDE = 2 * BLOCK
PEERS = [[z * 4 + (colour + 2 * z) % 4 for z in range(8)] for colour in range(4)]


def adam_moments(first, second, grad):
    return 0.9 * first + 0.1 * grad, 0.95 * second + 0.05 * grad * grad


def adam_update(param, first, second, step):
    upd = first / (1.0 - 0.9**step) / (jnp.sqrt(second / (1.0 - 0.95**step)) + 1e-08)
    return param - 0.1 * (upd + 0.1 * param)


def shift(x, axis, by):
    size = lax.axis_size(axis)
    return lax.ppermute(x, axis, [(i, (i + by) % size) for i in range(size)])


def other_core(x):
    return shift(x, "c", 1)


def exchange(x, axes):
    return lax.all_to_all(x, axes, 0, 0, tiled=True)


def pick(x, index, axis):
    return lax.dynamic_index_in_dim(x, index, axis, keepdims=False)


def together(*arrays):
    return lax.optimization_barrier(arrays)


def turned(x):
    return lax.ppermute(x, ("c", "x"), TURN)


def up(x):
    return shift(x, ("yh", "yl"), 1)


def down(x):
    return shift(x, ("yh", "yl"), -1)


def place():
    z, y = lax.axis_index("z"), lax.axis_index("yh") * 2 + lax.axis_index("yl")
    odd = lax.rem(z, 2)
    return z, y, odd, lax.rem(y + 2 * odd, 4)


def prepare_kernel(lengths, tokens, targets, out, inputs, goals, sems):
    copies = [
        pltpu.make_async_copy(tokens.at[0], inputs, sems.at[0]),
        pltpu.make_async_copy(targets.at[0], goals, sems.at[1]),
    ]
    for copy in copies:
        copy.start()
    z, y, _, colour = place()
    length = lengths[0, (z * 4 + y) * 2 + lax.axis_index("x")]
    valid = lax.broadcasted_iota(jnp.int32, inputs.shape, 0) < length
    copies[0].wait()
    out[:, WIDE : WIDE + D] = jnp.where(valid, inputs[...], jnp.zeros_like(inputs))
    copies[1].wait()
    for away, at in ((1, 0), (3, D + WIDE), (2, D + 2 * WIDE), (0, D + 3 * WIDE)):
        wanted = lax.rem(colour + away, 4)
        source = wanted // 2 * (2 * WIDE) + lax.rem(wanted, 2) * BLOCK
        for core in range(2):
            column = pl.multiple_of(source + core * WIDE, BLOCK)
            out[:, at + core * BLOCK : at + (core + 1) * BLOCK] = goals[
                :, pl.ds(column, BLOCK)
            ]


def prepare(lengths, tokens, targets):
    rows = tokens.shape[1]
    return pl.pallas_call(
        prepare_kernel,
        out_shape=jax.ShapeDtypeStruct((rows, D + 4 * WIDE), jnp.bfloat16),
        in_specs=[pl.BlockSpec(memory_space=pltpu.SMEM)]
        + [pl.BlockSpec(memory_space=pl.ANY)] * 2,
        out_specs=pl.BlockSpec(memory_space=pltpu.VMEM),
        scratch_shapes=[
            pltpu.VMEM((rows, D), jnp.bfloat16),
            pltpu.VMEM((rows, 4 * WIDE), jnp.bfloat16),
            pltpu.SemaphoreType.DMA((2,)),
        ],
        compiler_params=pltpu.CompilerParams(vmem_limit_bytes=60 * 2**20),
    )(lengths, tokens, targets)


def pack_kernel(param, weights):
    for slot in range(16):
        yl = slot // 2 % 2
        half = slice(yl * BLOCK, (yl + 1) * BLOCK)
        weights[slot] = param[:, half].astype(jnp.bfloat16)


def pack(param):
    whole = pl.BlockSpec(memory_space=pltpu.VMEM)
    return pl.pallas_call(
        pack_kernel,
        out_shape=jax.ShapeDtypeStruct((16, 32, BLOCK), jnp.bfloat16),
        in_specs=[whole],
        out_specs=whole,
        compiler_params=pltpu.CompilerParams(vmem_limit_bytes=60 * 2**20),
    )(param)


def pack_moments_kernel(lengths, first, second, moments):
    count = lax.fori_loop(0, lengths.shape[1], lambda i, t: t + lengths[0, i], 0)
    count = (count // 128).astype(jnp.float32)
    moments[0:32] = first[0].astype(jnp.bfloat16)
    moments[32:64] = second[0].astype(jnp.bfloat16)
    moments[64:80] = jnp.full((16, 8 * BLOCK), count).astype(jnp.bfloat16)


def pack_moments(lengths, first, second):
    whole = pl.BlockSpec(memory_space=pltpu.VMEM)
    return pl.pallas_call(
        pack_moments_kernel,
        out_shape=jax.ShapeDtypeStruct((80, 8 * BLOCK), jnp.bfloat16),
        in_specs=[pl.BlockSpec(memory_space=pltpu.SMEM), whole, whole],
        out_specs=whole,
        compiler_params=pltpu.CompilerParams(vmem_limit_bytes=16 * 2**20),
    )(lengths, first, second)


def finish_kernel(
    arrived, param, mom, first, second, new_param, new_mom, new_first, new_second
):
    _, _, odd, _ = place()
    h, c = lax.axis_index("h"), lax.axis_index("c")
    for yl in range(2):
        columns = slice(yl * BLOCK, (yl + 1) * BLOCK)
        total = jnp.zeros((32, BLOCK), jnp.float32)
        for group in range(4):
            yh = lax.rem(h + odd, 2)
            source = group // 2 * 16 + c * 8 + yh * 4 + yl * 2 + group % 2
            total += arrived[source, 0].astype(jnp.float32)
        pseudo = total / 4
        momentum = 0.9 * mom[:, columns] + pseudo
        new_mom[:, columns] = momentum
        new_param[:, columns] = param[:, columns] - 0.7 * (pseudo + 0.9 * momentum)
    for block in range(8):
        fh, core, fl = block // 4, block // 2 % 2, block % 2
        columns = slice(block * BLOCK, (block + 1) * BLOCK)
        source = h * 16 + core * 8 + lax.rem(fh + odd, 2) * 4 + fl * 2 + c
        moments = first[0, :, columns], second[0, :, columns]
        for step in range(STEPS):
            grad = arrived[source, 1 + step].astype(jnp.float32)
            moments = adam_moments(*moments, grad)
        new_first[0, :, columns], new_second[0, :, columns] = moments


def finish(*arrays):
    whole = pl.BlockSpec(memory_space=pltpu.VMEM)
    return pl.pallas_call(
        finish_kernel,
        out_shape=[jax.ShapeDtypeStruct(a.shape, a.dtype) for a in arrays[1:]],
        in_specs=[whole] * 5,
        out_specs=[whole] * 4,
        compiler_params=pltpu.CompilerParams(vmem_limit_bytes=16 * 2**20),
    )(*arrays)


def product_kernel(layout, last, core, weights, *refs):
    count = len(layout)
    blocks, refs = refs[:count], refs[count:]
    earlier, out, held, goals, total, sems = refs if len(refs) == 6 else (None, *refs)
    copies, row = [], 0
    for at, (rows, inputs_at, goals_at) in enumerate(layout):
        half = pl.multiple_of(goals_at + core[0] * BLOCK, BLOCK)
        sources = blocks[at].at[:, pl.ds(inputs_at, D)], blocks[at].at[:, pl.ds(half, BLOCK)]
        here = pl.ds(row, rows)
        for kind, (source, target) in enumerate(zip(sources, (held, goals))):
            copy = pltpu.make_async_copy(source, target.at[here], sems.at[kind, at])
            copy.start()
            copies.append(copy)
        row += rows
    if earlier is not None:
        total[...] = earlier[...]
    row = at = 0
    while at < count:
        size = 0
        while size < 512:
            copies[2 * at].wait()
            copies[2 * at + 1].wait()
            size += layout[at][0]
            at += 1
        inputs = held[row : row + size]
        goal = goals[row : row + size].astype(jnp.float32)
        outputs = jnp.dot(inputs, weights[...], preferred_element_type=jnp.float32)
        resid = (outputs * D ** (-0.5) - goal).astype(jnp.bfloat16)
        grad = lax.dot_general(
            resid, inputs, (((0,), (0,)), ((), ())), preferred_element_type=jnp.float32
        )
        if row == 0 and earlier is None:
            total[...] = grad
        else:
            total[...] += grad
        row += size
    if last:
        for z in range(8):
            out[z] = total[:, z * 256 : (z + 1) * 256].T.astype(jnp.bfloat16)
    else:
        out[...] = total[...]


def product(parts, core, weights, earlier=None, last=False):
    blocks = [block for block, _, _ in parts]
    layout = [(block.shape[0], *places) for block, *places in parts]
    rows = sum(block.shape[0] for block in blocks)
    whole = pl.BlockSpec(memory_space=pltpu.VMEM)
    args = [core, weights, *blocks]
    specs = [pl.BlockSpec(memory_space=pltpu.SMEM), whole]
    specs += [pl.BlockSpec(memory_space=pl.ANY)] * len(blocks)
    if earlier is not None:
        args.append(earlier)
        specs.append(whole)
    shape = ((8, 256, BLOCK), jnp.bfloat16) if last else ((BLOCK, D), jnp.float32)
    return pl.pallas_call(
        functools.partial(product_kernel, layout, last),
        out_shape=jax.ShapeDtypeStruct(*shape),
        in_specs=specs,
        out_specs=whole,
        scratch_shapes=[
            pltpu.VMEM((rows, D), jnp.bfloat16),
            pltpu.VMEM((rows, BLOCK), jnp.bfloat16),
            pltpu.VMEM((BLOCK, D), jnp.float32),
            pltpu.SemaphoreType.DMA((2, len(blocks))),
        ],
        compiler_params=pltpu.CompilerParams(vmem_limit_bytes=40 * 2**20),
        cost_estimate=pl.CostEstimate(
            flops=8 * rows * D * BLOCK, bytes_accessed=2 * rows * D, transcendentals=0
        ),
    )(*args)


def among_peers(x):
    axes = ("z", "yh", "yl")
    return lax.all_to_all(x, axes, 0, 0, axis_index_groups=PEERS, tiled=True)


def gathered(param):
    weights = jnp.broadcast_to(param.astype(jnp.bfloat16)[None], (8, 256, BLOCK))
    return among_peers(weights).reshape(D, BLOCK)


def reduced(grad):
    return jnp.sum(among_peers(grad).astype(jnp.float32), 0)


def per_device(tokens, targets, lengths, outer_param, outer_mom, first_mom, second_mom):
    c, x = lax.axis_index("c"), lax.axis_index("x")
    _, _, odd, colour = place()
    core = c.reshape(1).astype(jnp.int32)

    start = exchange(pack(outer_param), ("h", "yh", "yl", "x"))
    mine, start = together(prepare(lengths, tokens, targets), start)
    mine = turned(mine)
    theirs = other_core(mine)

    below, above = up(mine[:, : D + WIDE]), down(mine[:, WIDE : D + 2 * WIDE])
    half = mine.shape[0] // 2
    plane = jnp.concatenate(
        [mine[:, WIDE : WIDE + D], mine[:, D + 2 * WIDE : D + 3 * WIDE]], 1
    )

    start = start.reshape(2, 256, BLOCK)
    here = pick(start, colour // 2, 0)
    there = pick(start, 1 - colour // 2, 0)
    weights = jnp.where(
        (jnp.arange(8) % 2 == odd)[:, None, None], here[None], there[None]
    )
    weights = exchange(weights, "z").reshape(D, BLOCK)
    start = here.astype(jnp.float32)
    plane, weights = together(plane, weights)
    before, behind = shift(plane[:half], "z", 1), shift(plane[half:], "z", -1)

    moments, start = together(pack_moments(lengths, first_mom, second_mom), start)
    moments = lax.all_gather(turned(moments), ("yh", "yl", "c"), axis=0, tiled=True)
    column = colour // 2 * (2 * WIDE) + c * WIDE + colour % 2 * BLOCK
    moments = lax.dynamic_slice_in_dim(moments, column, BLOCK, 1).reshape(8, 80, BLOCK)

    near = [(block, WIDE, D + 3 * WIDE) for block in (mine, theirs)]
    near += [
        (block, 0, D)
        for block in (before, behind, other_core(before), other_core(behind))
    ]
    sides = [(block, WIDE, 0) for block in (below, other_core(below))]
    sides += [(block, 0, D) for block in (above, other_core(above))]
    grad = product(near, core, weights)
    grad = product(sides, core, weights, grad, last=True)

    first = moments[:, :32].reshape(256, BLOCK).astype(jnp.float32)
    second = moments[:, 32:64].reshape(256, BLOCK).astype(jnp.float32)
    coef = D ** (-0.5) / (128.0 * moments[0, 64, 0].astype(jnp.float32))
    grad = reduced(grad) * coef
    grads = [grad]
    first, second = adam_moments(first, second, grad)
    param = adam_update(start, first, second, PRIOR + 1)

    grad = product(near + sides, core, gathered(param), last=True)
    grad = reduced(grad) * coef
    grads.append(grad)
    first, second = adam_moments(first, second, grad)
    param = adam_update(param, first, second, PRIOR + 2)

    leaving = jnp.stack([start - param, *grads]).astype(jnp.bfloat16)
    leaving = jnp.moveaxis(leaving.reshape(3, 8, 32, BLOCK), 1, 0)
    leaving = jnp.broadcast_to(leaving[None], (4, 8, 3, 32, BLOCK))
    arrived = exchange(leaving.reshape(32, 3, 32, BLOCK), ("h", "c", "yh", "yl", "x"))
    return tuple(finish(arrived, outer_param, outer_mom, first_mom, second_mom))


def solution(mesh):
    fine = Mesh(
        mesh.devices.reshape(2, 2, 8, 2, 2, 2), ("h", "c", "z", "yh", "yl", "x")
    )
    group, fsdp = ("h", "c"), ("z", "yh", "yl", "x")
    in_specs = (
        P(group, fsdp, None),
        P(group, fsdp, None),
        P(group, None),
        P(fsdp, group),
        P(fsdp, group),
        P(group, fsdp, None),
        P(group, fsdp, None),
    )
    out_specs = (
        P(fsdp, group),
        P(fsdp, group),
        P(group, fsdp, None),
        P(group, fsdp, None),
    )
    return jax.shard_map(
        per_device, mesh=fine, in_specs=in_specs, out_specs=out_specs, check_vma=False
    )
```

```python
import functools

import jax
import jax.numpy as jnp
from jax import lax
from jax.experimental import pallas as pl
from jax.experimental.pallas import tpu as pltpu
from jax.sharding import Mesh
from jax.sharding import PartitionSpec as P

D = 2048
STEPS = 2
PRIOR = 1000
BLOCK = 128
TURN = [(0, 0), (1, 2), (2, 1), (3, 3)]
WIDE = 2 * BLOCK
PEERS = [[z * 4 + (colour + 2 * z) % 4 for z in range(8)] for colour in range(4)]


def adam_moments(first, second, grad):
    return 0.9 * first + 0.1 * grad, 0.95 * second + 0.05 * grad * grad


def adam_update(param, first, second, step):
    upd = first / (1.0 - 0.9**step) / (jnp.sqrt(second / (1.0 - 0.95**step)) + 1e-08)
    return param - 0.1 * (upd + 0.1 * param)


def shift(x, axis, by):
    size = lax.axis_size(axis)
    return lax.ppermute(x, axis, [(i, (i + by) % size) for i in range(size)])


def other_core(x):
    return shift(x, "c", 1)


def exchange(x, axes):
    return lax.all_to_all(x, axes, 0, 0, tiled=True)


def pick(x, index, axis):
    return lax.dynamic_index_in_dim(x, index, axis, keepdims=False)


def together(*arrays):
    return lax.optimization_barrier(arrays)


def turned(x):
    return lax.ppermute(x, ("c", "x"), TURN)


def up(x):
    return shift(x, ("yh", "yl"), 1)


def down(x):
    return shift(x, ("yh", "yl"), -1)


def place():
    z, y = lax.axis_index("z"), lax.axis_index("yh") * 2 + lax.axis_index("yl")
    odd = lax.rem(z, 2)
    return z, y, odd, lax.rem(y + 2 * odd, 4)


def prepare_kernel(first, lengths, tokens, targets, out, inputs, goals, sems):
    here = pl.ds(first, out.shape[0])
    copies = [
        pltpu.make_async_copy(tokens.at[0, here], inputs, sems.at[0]),
        pltpu.make_async_copy(targets.at[0, here], goals, sems.at[1]),
    ]
    for copy in copies:
        copy.start()
    z, y, _, colour = place()
    length = lengths[0, (z * 4 + y) * 2 + lax.axis_index("x")]
    valid = lax.broadcasted_iota(jnp.int32, inputs.shape, 0) + first < length
    copies[0].wait()
    out[:, WIDE : WIDE + D] = jnp.where(valid, inputs[...], jnp.zeros_like(inputs))
    copies[1].wait()
    for away, at in ((1, 0), (3, D + WIDE), (2, D + 2 * WIDE), (0, D + 3 * WIDE)):
        wanted = lax.rem(colour + away, 4)
        source = wanted // 2 * (2 * WIDE) + lax.rem(wanted, 2) * BLOCK
        for core in range(2):
            column = pl.multiple_of(source + core * WIDE, BLOCK)
            out[:, at + core * BLOCK : at + (core + 1) * BLOCK] = goals[
                :, pl.ds(column, BLOCK)
            ]


def prepare(first, lengths, tokens, targets):
    rows = tokens.shape[1] // 2
    return pl.pallas_call(
        functools.partial(prepare_kernel, first),
        out_shape=jax.ShapeDtypeStruct((rows, D + 4 * WIDE), jnp.bfloat16),
        in_specs=[pl.BlockSpec(memory_space=pltpu.SMEM)]
        + [pl.BlockSpec(memory_space=pl.ANY)] * 2,
        out_specs=pl.BlockSpec(memory_space=pltpu.VMEM),
        scratch_shapes=[
            pltpu.VMEM((rows, D), jnp.bfloat16),
            pltpu.VMEM((rows, 4 * WIDE), jnp.bfloat16),
            pltpu.SemaphoreType.DMA((2,)),
        ],
        compiler_params=pltpu.CompilerParams(vmem_limit_bytes=60 * 2**20),
    )(lengths, tokens, targets)


def pack_kernel(param, weights):
    for slot in range(16):
        yl = slot // 2 % 2
        half = slice(yl * BLOCK, (yl + 1) * BLOCK)
        weights[slot] = param[:, half].astype(jnp.bfloat16)


def pack(param):
    whole = pl.BlockSpec(memory_space=pltpu.VMEM)
    return pl.pallas_call(
        pack_kernel,
        out_shape=jax.ShapeDtypeStruct((16, 32, BLOCK), jnp.bfloat16),
        in_specs=[whole],
        out_specs=whole,
        compiler_params=pltpu.CompilerParams(vmem_limit_bytes=60 * 2**20),
    )(param)


def pack_moments_kernel(lengths, first, second, moments):
    _, _, odd, _ = place()
    count = lax.fori_loop(0, lengths.shape[1], lambda i, t: t + lengths[0, i], 0)
    count = (count // 128).astype(jnp.float32)
    for slot in range(16):
        core, yh, yl = slot // 8, slot // 4 % 2, slot // 2 % 2
        column = lax.rem(yh + odd, 2) * (2 * WIDE) + core * WIDE + yl * BLOCK
        columns = pl.ds(pl.multiple_of(column, BLOCK), BLOCK)
        moments[slot, 0:32] = first[0, :, columns].astype(jnp.bfloat16)
        moments[slot, 32:64] = second[0, :, columns].astype(jnp.bfloat16)
        moments[slot, 64:80] = jnp.full((16, BLOCK), count).astype(jnp.bfloat16)


def pack_moments(lengths, first, second):
    whole = pl.BlockSpec(memory_space=pltpu.VMEM)
    return pl.pallas_call(
        pack_moments_kernel,
        out_shape=jax.ShapeDtypeStruct((16, 80, BLOCK), jnp.bfloat16),
        in_specs=[pl.BlockSpec(memory_space=pltpu.SMEM), whole, whole],
        out_specs=whole,
        compiler_params=pltpu.CompilerParams(vmem_limit_bytes=16 * 2**20),
    )(lengths, first, second)


def finish_kernel(
    arrived, param, mom, first, second, new_param, new_mom, new_first, new_second
):
    _, _, odd, _ = place()
    h, c = lax.axis_index("h"), lax.axis_index("c")
    for yl in range(2):
        columns = slice(yl * BLOCK, (yl + 1) * BLOCK)
        total = jnp.zeros((32, BLOCK), jnp.float32)
        for group in range(4):
            yh = lax.rem(h + odd, 2)
            source = group // 2 * 16 + c * 8 + yh * 4 + yl * 2 + group % 2
            total += arrived[source, 0].astype(jnp.float32)
        pseudo = total / 4
        momentum = 0.9 * mom[:, columns] + pseudo
        new_mom[:, columns] = momentum
        new_param[:, columns] = param[:, columns] - 0.7 * (pseudo + 0.9 * momentum)
    for block in range(8):
        fh, core, fl = block // 4, block // 2 % 2, block % 2
        columns = slice(block * BLOCK, (block + 1) * BLOCK)
        source = h * 16 + core * 8 + lax.rem(fh + odd, 2) * 4 + fl * 2 + c
        moments = first[0, :, columns], second[0, :, columns]
        for step in range(STEPS):
            grad = arrived[source, 1 + step].astype(jnp.float32)
            moments = adam_moments(*moments, grad)
        new_first[0, :, columns], new_second[0, :, columns] = moments


def finish(*arrays):
    whole = pl.BlockSpec(memory_space=pltpu.VMEM)
    return pl.pallas_call(
        finish_kernel,
        out_shape=[jax.ShapeDtypeStruct(a.shape, a.dtype) for a in arrays[1:]],
        in_specs=[whole] * 5,
        out_specs=[whole] * 4,
        compiler_params=pltpu.CompilerParams(vmem_limit_bytes=16 * 2**20),
    )(*arrays)


def product_kernel(layout, last, core, weights, *refs):
    count = len(layout)
    blocks, refs = refs[:count], refs[count:]
    earlier, out, held, goals, total, sems = refs if len(refs) == 6 else (None, *refs)
    copies, row = [], 0
    for at, (rows, inputs_at, goals_at) in enumerate(layout):
        half = pl.multiple_of(goals_at + core[0] * BLOCK, BLOCK)
        sources = blocks[at].at[:, pl.ds(inputs_at, D)], blocks[at].at[:, pl.ds(half, BLOCK)]
        here = pl.ds(row, rows)
        for kind, (source, target) in enumerate(zip(sources, (held, goals))):
            copy = pltpu.make_async_copy(source, target.at[here], sems.at[kind, at])
            copy.start()
            copies.append(copy)
        row += rows
    if earlier is not None:
        total[...] = earlier[...]
    row = at = 0
    while at < count:
        size = 0
        while size < 512:
            copies[2 * at].wait()
            copies[2 * at + 1].wait()
            size += layout[at][0]
            at += 1
        inputs = held[row : row + size]
        goal = goals[row : row + size].astype(jnp.float32)
        outputs = jnp.dot(inputs, weights[...], preferred_element_type=jnp.float32)
        resid = (outputs * D ** (-0.5) - goal).astype(jnp.bfloat16)
        grad = lax.dot_general(
            resid, inputs, (((0,), (0,)), ((), ())), preferred_element_type=jnp.float32
        )
        if row == 0 and earlier is None:
            total[...] = grad
        else:
            total[...] += grad
        row += size
    if last:
        for z in range(8):
            out[z] = total[:, z * 256 : (z + 1) * 256].T.astype(jnp.bfloat16)
    else:
        out[...] = total[...]


def product(parts, core, weights, earlier=None, last=False):
    blocks = [block for block, _, _ in parts]
    layout = [(block.shape[0], *places) for block, *places in parts]
    rows = sum(block.shape[0] for block in blocks)
    whole = pl.BlockSpec(memory_space=pltpu.VMEM)
    args = [core, weights, *blocks]
    specs = [pl.BlockSpec(memory_space=pltpu.SMEM), whole]
    specs += [pl.BlockSpec(memory_space=pl.ANY)] * len(blocks)
    if earlier is not None:
        args.append(earlier)
        specs.append(whole)
    shape = ((8, 256, BLOCK), jnp.bfloat16) if last else ((BLOCK, D), jnp.float32)
    return pl.pallas_call(
        functools.partial(product_kernel, layout, last),
        out_shape=jax.ShapeDtypeStruct(*shape),
        in_specs=specs,
        out_specs=whole,
        scratch_shapes=[
            pltpu.VMEM((rows, D), jnp.bfloat16),
            pltpu.VMEM((rows, BLOCK), jnp.bfloat16),
            pltpu.VMEM((BLOCK, D), jnp.float32),
            pltpu.SemaphoreType.DMA((2, len(blocks))),
        ],
        compiler_params=pltpu.CompilerParams(vmem_limit_bytes=40 * 2**20),
        cost_estimate=pl.CostEstimate(
            flops=8 * rows * D * BLOCK, bytes_accessed=2 * rows * D, transcendentals=0
        ),
    )(*args)


def among_peers(x):
    axes = ("z", "yh", "yl")
    return lax.all_to_all(x, axes, 0, 0, axis_index_groups=PEERS, tiled=True)


def gathered(param):
    weights = jnp.broadcast_to(param.astype(jnp.bfloat16)[None], (8, 256, BLOCK))
    return among_peers(weights).reshape(D, BLOCK)


def reduced(grad):
    return jnp.sum(among_peers(grad).astype(jnp.float32), 0)


def per_device(tokens, targets, lengths, outer_param, outer_mom, first_mom, second_mom):
    c, x = lax.axis_index("c"), lax.axis_index("x")
    _, _, odd, colour = place()
    core = c.reshape(1).astype(jnp.int32)

    half = tokens.shape[1] // 2
    mine_a = turned(prepare(0, lengths, tokens, targets))
    start = exchange(pack(outer_param), ("h", "yh", "yl", "x"))
    mine_b, start = together(prepare(half, lengths, tokens, targets), start)
    mine_b = turned(mine_b)

    def both(*columns):
        return jnp.concatenate([mine_a[:, slice(*columns)], mine_b[:, slice(*columns)]], 0)

    below, above = up(both(0, D + WIDE)), down(both(WIDE, D + 2 * WIDE))

    def plane_of(mine):
        wanted = mine[:, D + 2 * WIDE : D + 3 * WIDE]
        return jnp.concatenate([mine[:, WIDE : WIDE + D], wanted], 1)

    start = start.reshape(2, 256, BLOCK)
    here = pick(start, colour // 2, 0)
    there = pick(start, 1 - colour // 2, 0)
    weights = jnp.where(
        (jnp.arange(8) % 2 == odd)[:, None, None], here[None], there[None]
    )
    weights = exchange(weights, "z").reshape(D, BLOCK)
    start = here.astype(jnp.float32)
    mine_a, mine_b, weights = together(mine_a, mine_b, weights)
    before, behind = plane_of(mine_a), plane_of(mine_b)
    before, behind = shift(before, "z", 1), shift(behind, "z", -1)

    moments, weights = together(pack_moments(lengths, first_mom, second_mom), weights)
    moments = exchange(moments, ("c", "yh", "yl", "x"))
    moments = pick(moments.reshape(2, 8, 80, BLOCK), x, 0)
    moments, before, behind = together(moments, before, behind)

    near = [(block, WIDE, D + 3 * WIDE) for block in (mine_a, mine_b)]
    near += [(other_core(block), WIDE, D + 3 * WIDE) for block in (mine_a, mine_b)]
    near += [
        (block, 0, D)
        for block in (before, behind, other_core(before), other_core(behind))
    ]
    sides = [(block, WIDE, 0) for block in (below, other_core(below))]
    sides += [(block, 0, D) for block in (above, other_core(above))]
    grad = product(near, core, weights)
    grad = product(sides, core, weights, grad, last=True)

    first = moments[:, :32].reshape(256, BLOCK).astype(jnp.float32)
    second = moments[:, 32:64].reshape(256, BLOCK).astype(jnp.float32)
    coef = D ** (-0.5) / (128.0 * moments[0, 64, 0].astype(jnp.float32))
    grad = reduced(grad) * coef
    grads = [grad]
    first, second = adam_moments(first, second, grad)
    param = adam_update(start, first, second, PRIOR + 1)

    grad = product(near + sides, core, gathered(param), last=True)
    grad = reduced(grad) * coef
    grads.append(grad)
    first, second = adam_moments(first, second, grad)
    param = adam_update(param, first, second, PRIOR + 2)

    leaving = jnp.stack([start - param, *grads]).astype(jnp.bfloat16)
    leaving = jnp.moveaxis(leaving.reshape(3, 8, 32, BLOCK), 1, 0)
    leaving = jnp.broadcast_to(leaving[None], (4, 8, 3, 32, BLOCK))
    arrived = exchange(leaving.reshape(32, 3, 32, BLOCK), ("h", "c", "yh", "yl", "x"))
    return tuple(finish(arrived, outer_param, outer_mom, first_mom, second_mom))


def solution(mesh):
    fine = Mesh(
        mesh.devices.reshape(2, 2, 8, 2, 2, 2), ("h", "c", "z", "yh", "yl", "x")
    )
    group, fsdp = ("h", "c"), ("z", "yh", "yl", "x")
    in_specs = (
        P(group, fsdp, None),
        P(group, fsdp, None),
        P(group, None),
        P(fsdp, group),
        P(fsdp, group),
        P(group, fsdp, None),
        P(group, fsdp, None),
    )
    out_specs = (
        P(fsdp, group),
        P(fsdp, group),
        P(group, fsdp, None),
        P(group, fsdp, None),
    )
    return jax.shard_map(
        per_device, mesh=fine, in_specs=in_specs, out_specs=out_specs, check_vma=False
    )
```

```python
import functools

import jax
import jax.numpy as jnp
from jax import lax
from jax.experimental import pallas as pl
from jax.experimental.pallas import tpu as pltpu
from jax.sharding import Mesh
from jax.sharding import PartitionSpec as P

D = 2048
STEPS = 2
PRIOR = 1000
BLOCK = 128
TURN = [(0, 0), (1, 2), (2, 1), (3, 3)]
WIDE = 2 * BLOCK
PEERS = [[z * 4 + (colour + 2 * z) % 4 for z in range(8)] for colour in range(4)]


def adam_moments(first, second, grad):
    return 0.9 * first + 0.1 * grad, 0.95 * second + 0.05 * grad * grad


def adam_update(param, first, second, step):
    upd = first / (1.0 - 0.9**step) / (jnp.sqrt(second / (1.0 - 0.95**step)) + 1e-08)
    return param - 0.1 * (upd + 0.1 * param)


def shift(x, axis, by):
    size = lax.axis_size(axis)
    return lax.ppermute(x, axis, [(i, (i + by) % size) for i in range(size)])


def other_core(x):
    return shift(x, "c", 1)


def exchange(x, axes):
    return lax.all_to_all(x, axes, 0, 0, tiled=True)


def pick(x, index, axis):
    return lax.dynamic_index_in_dim(x, index, axis, keepdims=False)


def together(*arrays):
    return lax.optimization_barrier(arrays)


def turned(x):
    return lax.ppermute(x, ("c", "x"), TURN)


def up(x):
    return shift(x, ("yh", "yl"), 1)


def down(x):
    return shift(x, ("yh", "yl"), -1)


def place():
    z, y = lax.axis_index("z"), lax.axis_index("yh") * 2 + lax.axis_index("yl")
    odd = lax.rem(z, 2)
    return z, y, odd, lax.rem(y + 2 * odd, 4)


def prepare_kernel(first, lengths, tokens, targets, out, inputs, goals, sems):
    here = pl.ds(first, out.shape[0])
    copies = [
        pltpu.make_async_copy(tokens.at[0, here], inputs, sems.at[0]),
        pltpu.make_async_copy(targets.at[0, here], goals, sems.at[1]),
    ]
    for copy in copies:
        copy.start()
    z, y, _, colour = place()
    length = lengths[0, (z * 4 + y) * 2 + lax.axis_index("x")]
    valid = lax.broadcasted_iota(jnp.int32, inputs.shape, 0) + first < length
    copies[0].wait()
    out[:, WIDE : WIDE + D] = jnp.where(valid, inputs[...], jnp.zeros_like(inputs))
    copies[1].wait()
    for away, at in ((1, 0), (3, D + WIDE), (2, D + 2 * WIDE), (0, D + 3 * WIDE)):
        wanted = lax.rem(colour + away, 4)
        source = wanted // 2 * (2 * WIDE) + lax.rem(wanted, 2) * BLOCK
        for core in range(2):
            column = pl.multiple_of(source + core * WIDE, BLOCK)
            out[:, at + core * BLOCK : at + (core + 1) * BLOCK] = goals[
                :, pl.ds(column, BLOCK)
            ]


def prepare(first, lengths, tokens, targets):
    rows = tokens.shape[1] // 2
    return pl.pallas_call(
        functools.partial(prepare_kernel, first),
        out_shape=jax.ShapeDtypeStruct((rows, D + 4 * WIDE), jnp.bfloat16),
        in_specs=[pl.BlockSpec(memory_space=pltpu.SMEM)]
        + [pl.BlockSpec(memory_space=pl.ANY)] * 2,
        out_specs=pl.BlockSpec(memory_space=pltpu.VMEM),
        scratch_shapes=[
            pltpu.VMEM((rows, D), jnp.bfloat16),
            pltpu.VMEM((rows, 4 * WIDE), jnp.bfloat16),
            pltpu.SemaphoreType.DMA((2,)),
        ],
        compiler_params=pltpu.CompilerParams(vmem_limit_bytes=60 * 2**20),
    )(lengths, tokens, targets)


def pack_kernel(param, weights):
    for slot in range(16):
        yl = slot // 2 % 2
        half = slice(yl * BLOCK, (yl + 1) * BLOCK)
        weights[slot] = param[:, half].astype(jnp.bfloat16)


def pack(param):
    whole = pl.BlockSpec(memory_space=pltpu.VMEM)
    return pl.pallas_call(
        pack_kernel,
        out_shape=jax.ShapeDtypeStruct((16, 32, BLOCK), jnp.bfloat16),
        in_specs=[whole],
        out_specs=whole,
        compiler_params=pltpu.CompilerParams(vmem_limit_bytes=60 * 2**20),
    )(param)


def pack_moments_kernel(lengths, first, second, moments):
    _, _, odd, _ = place()
    count = lax.fori_loop(0, lengths.shape[1], lambda i, t: t + lengths[0, i], 0)
    count = (count // 128).astype(jnp.float32)
    for slot in range(16):
        core, yh, yl = slot // 8, slot // 4 % 2, slot // 2 % 2
        column = lax.rem(yh + odd, 2) * (2 * WIDE) + core * WIDE + yl * BLOCK
        columns = pl.ds(pl.multiple_of(column, BLOCK), BLOCK)
        moments[slot, 0:32] = first[0, :, columns].astype(jnp.bfloat16)
        moments[slot, 32:64] = second[0, :, columns].astype(jnp.bfloat16)
        moments[slot, 64:80] = jnp.full((16, BLOCK), count).astype(jnp.bfloat16)


def pack_moments(lengths, first, second):
    whole = pl.BlockSpec(memory_space=pltpu.VMEM)
    return pl.pallas_call(
        pack_moments_kernel,
        out_shape=jax.ShapeDtypeStruct((16, 80, BLOCK), jnp.bfloat16),
        in_specs=[pl.BlockSpec(memory_space=pltpu.SMEM), whole, whole],
        out_specs=whole,
        compiler_params=pltpu.CompilerParams(vmem_limit_bytes=16 * 2**20),
    )(lengths, first, second)


def finish_kernel(
    arrived, param, mom, first, second, new_param, new_mom, new_first, new_second
):
    _, _, odd, _ = place()
    h, c = lax.axis_index("h"), lax.axis_index("c")
    for yl in range(2):
        columns = slice(yl * BLOCK, (yl + 1) * BLOCK)
        total = jnp.zeros((32, BLOCK), jnp.float32)
        for group in range(4):
            yh = lax.rem(h + odd, 2)
            source = group // 2 * 16 + c * 8 + yh * 4 + yl * 2 + group % 2
            total += arrived[source, 0].astype(jnp.float32)
        pseudo = total / 4
        momentum = 0.9 * mom[:, columns] + pseudo
        new_mom[:, columns] = momentum
        new_param[:, columns] = param[:, columns] - 0.7 * (pseudo + 0.9 * momentum)
    for block in range(8):
        fh, core, fl = block // 4, block // 2 % 2, block % 2
        columns = slice(block * BLOCK, (block + 1) * BLOCK)
        source = h * 16 + core * 8 + lax.rem(fh + odd, 2) * 4 + fl * 2 + c
        moments = first[0, :, columns], second[0, :, columns]
        for step in range(STEPS):
            grad = arrived[source, 1 + step].astype(jnp.float32)
            moments = adam_moments(*moments, grad)
        new_first[0, :, columns], new_second[0, :, columns] = moments


def finish(*arrays):
    whole = pl.BlockSpec(memory_space=pltpu.VMEM)
    return pl.pallas_call(
        finish_kernel,
        out_shape=[jax.ShapeDtypeStruct(a.shape, a.dtype) for a in arrays[1:]],
        in_specs=[whole] * 5,
        out_specs=[whole] * 4,
        compiler_params=pltpu.CompilerParams(vmem_limit_bytes=16 * 2**20),
    )(*arrays)


def product_kernel(layout, last, core, weights, *refs):
    count = len(layout)
    blocks, refs = refs[:count], refs[count:]
    earlier, out, held, goals, total, sems = refs if len(refs) == 6 else (None, *refs)
    copies, row = [], 0
    for at, (rows, inputs_at, goals_at) in enumerate(layout):
        half = pl.multiple_of(goals_at + core[0] * BLOCK, BLOCK)
        sources = blocks[at].at[:, pl.ds(inputs_at, D)], blocks[at].at[:, pl.ds(half, BLOCK)]
        here = pl.ds(row, rows)
        for kind, (source, target) in enumerate(zip(sources, (held, goals))):
            copy = pltpu.make_async_copy(source, target.at[here], sems.at[kind, at])
            copy.start()
            copies.append(copy)
        row += rows
    if earlier is not None:
        total[...] = earlier[...]
    row = at = 0
    while at < count:
        size = 0
        while size < 512:
            copies[2 * at].wait()
            copies[2 * at + 1].wait()
            size += layout[at][0]
            at += 1
        inputs = held[row : row + size]
        goal = goals[row : row + size].astype(jnp.float32)
        outputs = jnp.dot(inputs, weights[...], preferred_element_type=jnp.float32)
        resid = (outputs * D ** (-0.5) - goal).astype(jnp.bfloat16)
        grad = lax.dot_general(
            resid, inputs, (((0,), (0,)), ((), ())), preferred_element_type=jnp.float32
        )
        if row == 0 and earlier is None:
            total[...] = grad
        else:
            total[...] += grad
        row += size
    if last:
        for z in range(8):
            out[z] = total[:, z * 256 : (z + 1) * 256].T.astype(jnp.bfloat16)
    else:
        out[...] = total[...]


def product(parts, core, weights, earlier=None, last=False):
    blocks = [block for block, _, _ in parts]
    layout = [(block.shape[0], *places) for block, *places in parts]
    rows = sum(block.shape[0] for block in blocks)
    whole = pl.BlockSpec(memory_space=pltpu.VMEM)
    args = [core, weights, *blocks]
    specs = [pl.BlockSpec(memory_space=pltpu.SMEM), whole]
    specs += [pl.BlockSpec(memory_space=pl.ANY)] * len(blocks)
    if earlier is not None:
        args.append(earlier)
        specs.append(whole)
    shape = ((8, 256, BLOCK), jnp.bfloat16) if last else ((BLOCK, D), jnp.float32)
    return pl.pallas_call(
        functools.partial(product_kernel, layout, last),
        out_shape=jax.ShapeDtypeStruct(*shape),
        in_specs=specs,
        out_specs=whole,
        scratch_shapes=[
            pltpu.VMEM((rows, D), jnp.bfloat16),
            pltpu.VMEM((rows, BLOCK), jnp.bfloat16),
            pltpu.VMEM((BLOCK, D), jnp.float32),
            pltpu.SemaphoreType.DMA((2, len(blocks))),
        ],
        compiler_params=pltpu.CompilerParams(vmem_limit_bytes=40 * 2**20),
        cost_estimate=pl.CostEstimate(
            flops=8 * rows * D * BLOCK, bytes_accessed=2 * rows * D, transcendentals=0
        ),
    )(*args)


def among_peers(x):
    axes = ("z", "yh", "yl")
    return lax.all_to_all(x, axes, 0, 0, axis_index_groups=PEERS, tiled=True)


def gathered(param):
    weights = jnp.broadcast_to(param.astype(jnp.bfloat16)[None], (8, 256, BLOCK))
    return among_peers(weights).reshape(D, BLOCK)


def reduced(grad):
    return jnp.sum(among_peers(grad).astype(jnp.float32), 0)


def per_device(tokens, targets, lengths, outer_param, outer_mom, first_mom, second_mom):
    c, x = lax.axis_index("c"), lax.axis_index("x")
    _, _, odd, colour = place()
    core = c.reshape(1).astype(jnp.int32)

    half = tokens.shape[1] // 2
    mine_a = turned(prepare(0, lengths, tokens, targets))
    start = exchange(pack(outer_param), ("h", "yh", "yl", "x"))
    mine_b = turned(prepare(half, lengths, tokens, targets))

    def both(*columns):
        return jnp.concatenate([mine_a[:, slice(*columns)], mine_b[:, slice(*columns)]], 0)

    below, above = up(both(0, D + WIDE)), down(both(WIDE, D + 2 * WIDE))

    def plane_of(mine):
        wanted = mine[:, D + 2 * WIDE : D + 3 * WIDE]
        return jnp.concatenate([mine[:, WIDE : WIDE + D], wanted], 1)

    start = start.reshape(2, 256, BLOCK)
    here = pick(start, colour // 2, 0)
    there = pick(start, 1 - colour // 2, 0)
    weights = jnp.where(
        (jnp.arange(8) % 2 == odd)[:, None, None], here[None], there[None]
    )
    weights = exchange(weights, "z").reshape(D, BLOCK)
    start = here.astype(jnp.float32)
    mine_a, mine_b, weights = together(mine_a, mine_b, weights)
    before, behind = plane_of(mine_a), plane_of(mine_b)
    before, behind = shift(before, "z", 1), shift(behind, "z", -1)

    moments, weights = together(pack_moments(lengths, first_mom, second_mom), weights)
    moments = exchange(moments, ("c", "yh", "yl", "x"))
    moments = pick(moments.reshape(2, 8, 80, BLOCK), x, 0)
    moments, before, behind = together(moments, before, behind)

    near = [(block, WIDE, D + 3 * WIDE) for block in (mine_a, mine_b)]
    near += [(other_core(block), WIDE, D + 3 * WIDE) for block in (mine_a, mine_b)]
    near += [
        (block, 0, D)
        for block in (before, behind, other_core(before), other_core(behind))
    ]
    sides = [(block, WIDE, 0) for block in (below, other_core(below))]
    sides += [(block, 0, D) for block in (above, other_core(above))]
    grad = product(near, core, weights)
    grad = product(sides, core, weights, grad, last=True)

    first = moments[:, :32].reshape(256, BLOCK).astype(jnp.float32)
    second = moments[:, 32:64].reshape(256, BLOCK).astype(jnp.float32)
    coef = D ** (-0.5) / (128.0 * moments[0, 64, 0].astype(jnp.float32))
    grad = reduced(grad) * coef
    grads = [grad]
    first, second = adam_moments(first, second, grad)
    param = adam_update(start, first, second, PRIOR + 1)

    grad = product(near + sides, core, gathered(param), last=True)
    grad = reduced(grad) * coef
    grads.append(grad)
    first, second = adam_moments(first, second, grad)
    param = adam_update(param, first, second, PRIOR + 2)

    leaving = jnp.stack([start - param, *grads]).astype(jnp.bfloat16)
    leaving = jnp.moveaxis(leaving.reshape(3, 8, 32, BLOCK), 1, 0)
    leaving = jnp.broadcast_to(leaving[None], (4, 8, 3, 32, BLOCK))
    arrived = exchange(leaving.reshape(32, 3, 32, BLOCK), ("h", "c", "yh", "yl", "x"))
    return tuple(finish(arrived, outer_param, outer_mom, first_mom, second_mom))


def solution(mesh):
    fine = Mesh(
        mesh.devices.reshape(2, 2, 8, 2, 2, 2), ("h", "c", "z", "yh", "yl", "x")
    )
    group, fsdp = ("h", "c"), ("z", "yh", "yl", "x")
    in_specs = (
        P(group, fsdp, None),
        P(group, fsdp, None),
        P(group, None),
        P(fsdp, group),
        P(fsdp, group),
        P(group, fsdp, None),
        P(group, fsdp, None),
    )
    out_specs = (
        P(fsdp, group),
        P(fsdp, group),
        P(group, fsdp, None),
        P(group, fsdp, None),
    )
    return jax.shard_map(
        per_device, mesh=fine, in_specs=in_specs, out_specs=out_specs, check_vma=False
    )
```

```python
import functools

import jax
import jax.numpy as jnp
from jax import lax
from jax.experimental import pallas as pl
from jax.experimental.pallas import tpu as pltpu
from jax.sharding import Mesh
from jax.sharding import PartitionSpec as P

D = 2048
STEPS = 2
PRIOR = 1000
BLOCK = 128
TURN = [(0, 0), (1, 2), (2, 1), (3, 3)]
WIDE = 2 * BLOCK
PEERS = [[z * 4 + (colour + 2 * z) % 4 for z in range(8)] for colour in range(4)]


def adam_moments(first, second, grad):
    return 0.9 * first + 0.1 * grad, 0.95 * second + 0.05 * grad * grad


def adam_update(param, first, second, step):
    upd = first / (1.0 - 0.9**step) / (jnp.sqrt(second / (1.0 - 0.95**step)) + 1e-08)
    return param - 0.1 * (upd + 0.1 * param)


def shift(x, axis, by):
    size = lax.axis_size(axis)
    return lax.ppermute(x, axis, [(i, (i + by) % size) for i in range(size)])


def other_core(x):
    return shift(x, "c", 1)


def exchange(x, axes):
    return lax.all_to_all(x, axes, 0, 0, tiled=True)


def pick(x, index, axis):
    return lax.dynamic_index_in_dim(x, index, axis, keepdims=False)


def together(*arrays):
    return lax.optimization_barrier(arrays)


def turned(x):
    return lax.ppermute(x, ("c", "x"), TURN)


def up(x):
    return shift(x, ("yh", "yl"), 1)


def down(x):
    return shift(x, ("yh", "yl"), -1)


def place():
    z, y = lax.axis_index("z"), lax.axis_index("yh") * 2 + lax.axis_index("yl")
    odd = lax.rem(z, 2)
    return z, y, odd, lax.rem(y + 2 * odd, 4)


def prepare_kernel(first, lengths, tokens, targets, out, inputs, goals, sems):
    here = pl.ds(first, out.shape[0])
    copies = [
        pltpu.make_async_copy(tokens.at[0, here], inputs, sems.at[0]),
        pltpu.make_async_copy(targets.at[0, here], goals, sems.at[1]),
    ]
    for copy in copies:
        copy.start()
    z, y, _, colour = place()
    length = lengths[0, (z * 4 + y) * 2 + lax.axis_index("x")]
    valid = lax.broadcasted_iota(jnp.int32, inputs.shape, 0) + first < length
    copies[0].wait()
    out[:, WIDE : WIDE + D] = jnp.where(valid, inputs[...], jnp.zeros_like(inputs))
    copies[1].wait()
    for away, at in ((1, 0), (3, D + WIDE), (2, D + 2 * WIDE), (0, D + 3 * WIDE)):
        wanted = lax.rem(colour + away, 4)
        source = wanted // 2 * (2 * WIDE) + lax.rem(wanted, 2) * BLOCK
        for core in range(2):
            column = pl.multiple_of(source + core * WIDE, BLOCK)
            out[:, at + core * BLOCK : at + (core + 1) * BLOCK] = goals[
                :, pl.ds(column, BLOCK)
            ]


def prepare(first, lengths, tokens, targets):
    rows = tokens.shape[1] // 2
    return pl.pallas_call(
        functools.partial(prepare_kernel, first),
        out_shape=jax.ShapeDtypeStruct((rows, D + 4 * WIDE), jnp.bfloat16),
        in_specs=[pl.BlockSpec(memory_space=pltpu.SMEM)]
        + [pl.BlockSpec(memory_space=pl.ANY)] * 2,
        out_specs=pl.BlockSpec(memory_space=pltpu.VMEM),
        scratch_shapes=[
            pltpu.VMEM((rows, D), jnp.bfloat16),
            pltpu.VMEM((rows, 4 * WIDE), jnp.bfloat16),
            pltpu.SemaphoreType.DMA((2,)),
        ],
        compiler_params=pltpu.CompilerParams(vmem_limit_bytes=60 * 2**20),
    )(lengths, tokens, targets)


def pack_kernel(param, weights):
    for slot in range(16):
        yl = slot // 2 % 2
        half = slice(yl * BLOCK, (yl + 1) * BLOCK)
        weights[slot] = param[:, half].astype(jnp.bfloat16)


def pack(param):
    whole = pl.BlockSpec(memory_space=pltpu.VMEM)
    return pl.pallas_call(
        pack_kernel,
        out_shape=jax.ShapeDtypeStruct((16, 32, BLOCK), jnp.bfloat16),
        in_specs=[whole],
        out_specs=whole,
        compiler_params=pltpu.CompilerParams(vmem_limit_bytes=60 * 2**20),
    )(param)


def pack_moments_kernel(lengths, first, second, moments):
    _, _, odd, _ = place()
    count = lax.fori_loop(0, lengths.shape[1], lambda i, t: t + lengths[0, i], 0)
    count = (count // 128).astype(jnp.float32)
    for slot in range(16):
        core, yh, yl = slot // 8, slot // 4 % 2, slot // 2 % 2
        column = lax.rem(yh + odd, 2) * (2 * WIDE) + core * WIDE + yl * BLOCK
        columns = pl.ds(pl.multiple_of(column, BLOCK), BLOCK)
        moments[slot, 0:32] = first[0, :, columns].astype(jnp.bfloat16)
        moments[slot, 32:64] = second[0, :, columns].astype(jnp.bfloat16)
        moments[slot, 64:80] = jnp.full((16, BLOCK), count).astype(jnp.bfloat16)


def pack_moments(lengths, first, second):
    whole = pl.BlockSpec(memory_space=pltpu.VMEM)
    return pl.pallas_call(
        pack_moments_kernel,
        out_shape=jax.ShapeDtypeStruct((16, 80, BLOCK), jnp.bfloat16),
        in_specs=[pl.BlockSpec(memory_space=pltpu.SMEM), whole, whole],
        out_specs=whole,
        compiler_params=pltpu.CompilerParams(vmem_limit_bytes=16 * 2**20),
    )(lengths, first, second)


def finish_kernel(
    arrived, param, mom, first, second, new_param, new_mom, new_first, new_second
):
    _, _, odd, _ = place()
    h, c = lax.axis_index("h"), lax.axis_index("c")
    for yl in range(2):
        columns = slice(yl * BLOCK, (yl + 1) * BLOCK)
        total = jnp.zeros((32, BLOCK), jnp.float32)
        for group in range(4):
            yh = lax.rem(h + odd, 2)
            source = group // 2 * 16 + c * 8 + yh * 4 + yl * 2 + group % 2
            total += arrived[source, 0].astype(jnp.float32)
        pseudo = total / 4
        momentum = 0.9 * mom[:, columns] + pseudo
        new_mom[:, columns] = momentum
        new_param[:, columns] = param[:, columns] - 0.7 * (pseudo + 0.9 * momentum)
    for block in range(8):
        fh, core, fl = block // 4, block // 2 % 2, block % 2
        columns = slice(block * BLOCK, (block + 1) * BLOCK)
        source = h * 16 + core * 8 + lax.rem(fh + odd, 2) * 4 + fl * 2 + c
        moments = first[0, :, columns], second[0, :, columns]
        for step in range(STEPS):
            grad = arrived[source, 1 + step].astype(jnp.float32)
            moments = adam_moments(*moments, grad)
        new_first[0, :, columns], new_second[0, :, columns] = moments


def finish(*arrays):
    whole = pl.BlockSpec(memory_space=pltpu.VMEM)
    return pl.pallas_call(
        finish_kernel,
        out_shape=[jax.ShapeDtypeStruct(a.shape, a.dtype) for a in arrays[1:]],
        in_specs=[whole] * 5,
        out_specs=[whole] * 4,
        compiler_params=pltpu.CompilerParams(vmem_limit_bytes=16 * 2**20),
    )(*arrays)


def product_kernel(layout, last, core, weights, *refs):
    count = len(layout)
    blocks, refs = refs[:count], refs[count:]
    earlier, out, held, goals, total, sems = refs if len(refs) == 6 else (None, *refs)
    copies, row = [], 0
    for at, (rows, inputs_at, goals_at) in enumerate(layout):
        half = pl.multiple_of(goals_at + core[0] * BLOCK, BLOCK)
        sources = blocks[at].at[:, pl.ds(inputs_at, D)], blocks[at].at[:, pl.ds(half, BLOCK)]
        here = pl.ds(row, rows)
        for kind, (source, target) in enumerate(zip(sources, (held, goals))):
            copy = pltpu.make_async_copy(source, target.at[here], sems.at[kind, at])
            copy.start()
            copies.append(copy)
        row += rows
    if earlier is not None:
        total[...] = earlier[...]
    row = at = 0
    while at < count:
        size = 0
        while size < 512:
            copies[2 * at].wait()
            copies[2 * at + 1].wait()
            size += layout[at][0]
            at += 1
        inputs = held[row : row + size]
        goal = goals[row : row + size].astype(jnp.float32)
        outputs = jnp.dot(inputs, weights[...], preferred_element_type=jnp.float32)
        resid = (outputs * D ** (-0.5) - goal).astype(jnp.bfloat16)
        grad = lax.dot_general(
            resid, inputs, (((0,), (0,)), ((), ())), preferred_element_type=jnp.float32
        )
        if row == 0 and earlier is None:
            total[...] = grad
        else:
            total[...] += grad
        row += size
    if last:
        for z in range(8):
            out[z] = total[:, z * 256 : (z + 1) * 256].T.astype(jnp.bfloat16)
    else:
        out[...] = total[...]


def product(parts, core, weights, earlier=None, last=False):
    blocks = [block for block, _, _ in parts]
    layout = [(block.shape[0], *places) for block, *places in parts]
    rows = sum(block.shape[0] for block in blocks)
    whole = pl.BlockSpec(memory_space=pltpu.VMEM)
    args = [core, weights, *blocks]
    specs = [pl.BlockSpec(memory_space=pltpu.SMEM), whole]
    specs += [pl.BlockSpec(memory_space=pl.ANY)] * len(blocks)
    if earlier is not None:
        args.append(earlier)
        specs.append(whole)
    shape = ((8, 256, BLOCK), jnp.bfloat16) if last else ((BLOCK, D), jnp.float32)
    return pl.pallas_call(
        functools.partial(product_kernel, layout, last),
        out_shape=jax.ShapeDtypeStruct(*shape),
        in_specs=specs,
        out_specs=whole,
        scratch_shapes=[
            pltpu.VMEM((rows, D), jnp.bfloat16),
            pltpu.VMEM((rows, BLOCK), jnp.bfloat16),
            pltpu.VMEM((BLOCK, D), jnp.float32),
            pltpu.SemaphoreType.DMA((2, len(blocks))),
        ],
        compiler_params=pltpu.CompilerParams(vmem_limit_bytes=40 * 2**20),
        cost_estimate=pl.CostEstimate(
            flops=8 * rows * D * BLOCK, bytes_accessed=2 * rows * D, transcendentals=0
        ),
    )(*args)


def among_peers(x):
    axes = ("z", "yh", "yl")
    return lax.all_to_all(x, axes, 0, 0, axis_index_groups=PEERS, tiled=True)


def gathered(param):
    weights = jnp.broadcast_to(param.astype(jnp.bfloat16)[None], (8, 256, BLOCK))
    return among_peers(weights).reshape(D, BLOCK)


def reduced(grad):
    return jnp.sum(among_peers(grad).astype(jnp.float32), 0)


def per_device(tokens, targets, lengths, outer_param, outer_mom, first_mom, second_mom):
    c, x = lax.axis_index("c"), lax.axis_index("x")
    _, _, odd, colour = place()
    core = c.reshape(1).astype(jnp.int32)

    half = tokens.shape[1] // 2
    mine_a = turned(prepare(0, lengths, tokens, targets))
    start = exchange(pack(outer_param), ("h", "yh", "yl", "x"))
    mine_b = turned(prepare(half, lengths, tokens, targets))

    def both(*columns):
        return jnp.concatenate([mine_a[:, slice(*columns)], mine_b[:, slice(*columns)]], 0)

    below, above = up(both(0, D + WIDE)), down(both(WIDE, D + 2 * WIDE))

    def plane_of(mine):
        wanted = mine[:, D + 2 * WIDE : D + 3 * WIDE]
        return jnp.concatenate([mine[:, WIDE : WIDE + D], wanted], 1)

    start = start.reshape(2, 256, BLOCK)
    here = pick(start, colour // 2, 0)
    there = pick(start, 1 - colour // 2, 0)
    weights = jnp.where(
        (jnp.arange(8) % 2 == odd)[:, None, None], here[None], there[None]
    )
    weights = exchange(weights, "z").reshape(D, BLOCK)
    start = here.astype(jnp.float32)
    mine_a, mine_b, weights = together(mine_a, mine_b, weights)
    before, behind = plane_of(mine_a), plane_of(mine_b)
    before, behind = shift(before, "z", 1), shift(behind, "z", -1)

    moments, weights = together(pack_moments(lengths, first_mom, second_mom), weights)
    moments = exchange(moments, ("c", "yh", "yl", "x"))
    moments, above = together(moments, above)
    moments = pick(moments.reshape(2, 8, 80, BLOCK), x, 0)

    near = [(block, WIDE, D + 3 * WIDE) for block in (mine_a, mine_b)]
    near += [(other_core(block), WIDE, D + 3 * WIDE) for block in (mine_a, mine_b)]
    near += [
        (block, 0, D)
        for block in (before, behind, other_core(before), other_core(behind))
    ]
    sides = [(block, WIDE, 0) for block in (below, other_core(below))]
    sides += [(block, 0, D) for block in (above, other_core(above))]
    grad = product(near, core, weights)
    grad = product(sides, core, weights, grad, last=True)

    first = moments[:, :32].reshape(256, BLOCK).astype(jnp.float32)
    second = moments[:, 32:64].reshape(256, BLOCK).astype(jnp.float32)
    coef = D ** (-0.5) / (128.0 * moments[0, 64, 0].astype(jnp.float32))
    grad = reduced(grad) * coef
    grads = [grad]
    first, second = adam_moments(first, second, grad)
    param = adam_update(start, first, second, PRIOR + 1)

    grad = product(near + sides, core, gathered(param), last=True)
    grad = reduced(grad) * coef
    grads.append(grad)
    first, second = adam_moments(first, second, grad)
    param = adam_update(param, first, second, PRIOR + 2)

    leaving = jnp.stack([start - param, *grads]).astype(jnp.bfloat16)
    leaving = jnp.moveaxis(leaving.reshape(3, 8, 32, BLOCK), 1, 0)
    leaving = jnp.broadcast_to(leaving[None], (4, 8, 3, 32, BLOCK))
    arrived = exchange(leaving.reshape(32, 3, 32, BLOCK), ("h", "c", "yh", "yl", "x"))
    return tuple(finish(arrived, outer_param, outer_mom, first_mom, second_mom))


def solution(mesh):
    fine = Mesh(
        mesh.devices.reshape(2, 2, 8, 2, 2, 2), ("h", "c", "z", "yh", "yl", "x")
    )
    group, fsdp = ("h", "c"), ("z", "yh", "yl", "x")
    in_specs = (
        P(group, fsdp, None),
        P(group, fsdp, None),
        P(group, None),
        P(fsdp, group),
        P(fsdp, group),
        P(group, fsdp, None),
        P(group, fsdp, None),
    )
    out_specs = (
        P(fsdp, group),
        P(fsdp, group),
        P(group, fsdp, None),
        P(group, fsdp, None),
    )
    return jax.shard_map(
        per_device, mesh=fine, in_specs=in_specs, out_specs=out_specs, check_vma=False
    )
```

```python
import functools

import jax
import jax.numpy as jnp
from jax import lax
from jax.experimental import pallas as pl
from jax.experimental.pallas import tpu as pltpu
from jax.sharding import Mesh
from jax.sharding import PartitionSpec as P

D = 2048
STEPS = 2
PRIOR = 1000
BLOCK = 128
TURN = [(0, 0), (1, 2), (2, 1), (3, 3)]
WIDE = 2 * BLOCK
PEERS = [[z * 4 + (colour + 2 * z) % 4 for z in range(8)] for colour in range(4)]


def adam_moments(first, second, grad):
    return 0.9 * first + 0.1 * grad, 0.95 * second + 0.05 * grad * grad


def adam_update(param, first, second, step):
    upd = first / (1.0 - 0.9**step) / (jnp.sqrt(second / (1.0 - 0.95**step)) + 1e-08)
    return param - 0.1 * (upd + 0.1 * param)


def shift(x, axis, by):
    size = lax.axis_size(axis)
    return lax.ppermute(x, axis, [(i, (i + by) % size) for i in range(size)])


def other_core(x):
    return shift(x, "c", 1)


def exchange(x, axes):
    return lax.all_to_all(x, axes, 0, 0, tiled=True)


def pick(x, index, axis):
    return lax.dynamic_index_in_dim(x, index, axis, keepdims=False)


def together(*arrays):
    return lax.optimization_barrier(arrays)


def turned(x):
    return lax.ppermute(x, ("c", "x"), TURN)


def up(x):
    return shift(x, ("yh", "yl"), 1)


def down(x):
    return shift(x, ("yh", "yl"), -1)


def place():
    z, y = lax.axis_index("z"), lax.axis_index("yh") * 2 + lax.axis_index("yl")
    odd = lax.rem(z, 2)
    return z, y, odd, lax.rem(y + 2 * odd, 4)


def prepare_kernel(first, lengths, tokens, targets, out, inputs, goals, sems):
    here = pl.ds(first, out.shape[0])
    copies = [
        pltpu.make_async_copy(tokens.at[0, here], inputs, sems.at[0]),
        pltpu.make_async_copy(targets.at[0, here], goals, sems.at[1]),
    ]
    for copy in copies:
        copy.start()
    z, y, _, colour = place()
    length = lengths[0, (z * 4 + y) * 2 + lax.axis_index("x")]
    valid = lax.broadcasted_iota(jnp.int32, inputs.shape, 0) + first < length
    copies[0].wait()
    out[:, WIDE : WIDE + D] = jnp.where(valid, inputs[...], jnp.zeros_like(inputs))
    copies[1].wait()
    for away, at in ((1, 0), (3, D + WIDE), (2, D + 2 * WIDE), (0, D + 3 * WIDE)):
        wanted = lax.rem(colour + away, 4)
        source = wanted // 2 * (2 * WIDE) + lax.rem(wanted, 2) * BLOCK
        for core in range(2):
            column = pl.multiple_of(source + core * WIDE, BLOCK)
            out[:, at + core * BLOCK : at + (core + 1) * BLOCK] = goals[
                :, pl.ds(column, BLOCK)
            ]


def prepare(first, lengths, tokens, targets):
    rows = tokens.shape[1] // 2
    return pl.pallas_call(
        functools.partial(prepare_kernel, first),
        out_shape=jax.ShapeDtypeStruct((rows, D + 4 * WIDE), jnp.bfloat16),
        in_specs=[pl.BlockSpec(memory_space=pltpu.SMEM)]
        + [pl.BlockSpec(memory_space=pl.ANY)] * 2,
        out_specs=pl.BlockSpec(memory_space=pltpu.VMEM),
        scratch_shapes=[
            pltpu.VMEM((rows, D), jnp.bfloat16),
            pltpu.VMEM((rows, 4 * WIDE), jnp.bfloat16),
            pltpu.SemaphoreType.DMA((2,)),
        ],
        compiler_params=pltpu.CompilerParams(vmem_limit_bytes=60 * 2**20),
    )(lengths, tokens, targets)


def pack_kernel(param, weights):
    for slot in range(16):
        yl = slot // 2 % 2
        half = slice(yl * BLOCK, (yl + 1) * BLOCK)
        weights[slot] = param[:, half].astype(jnp.bfloat16)


def pack(param):
    whole = pl.BlockSpec(memory_space=pltpu.VMEM)
    return pl.pallas_call(
        pack_kernel,
        out_shape=jax.ShapeDtypeStruct((16, 32, BLOCK), jnp.bfloat16),
        in_specs=[whole],
        out_specs=whole,
        compiler_params=pltpu.CompilerParams(vmem_limit_bytes=60 * 2**20),
    )(param)


def pack_moments_kernel(lengths, first, second, moments):
    _, _, odd, _ = place()
    count = lax.fori_loop(0, lengths.shape[1], lambda i, t: t + lengths[0, i], 0)
    count = (count // 128).astype(jnp.float32)
    for slot in range(16):
        core, yh, yl = slot // 8, slot // 4 % 2, slot // 2 % 2
        column = lax.rem(yh + odd, 2) * (2 * WIDE) + core * WIDE + yl * BLOCK
        columns = pl.ds(pl.multiple_of(column, BLOCK), BLOCK)
        moments[slot, 0:32] = first[0, :, columns].astype(jnp.bfloat16)
        moments[slot, 32:64] = second[0, :, columns].astype(jnp.bfloat16)
        moments[slot, 64:80] = jnp.full((16, BLOCK), count).astype(jnp.bfloat16)


def pack_moments(lengths, first, second):
    whole = pl.BlockSpec(memory_space=pltpu.VMEM)
    return pl.pallas_call(
        pack_moments_kernel,
        out_shape=jax.ShapeDtypeStruct((16, 80, BLOCK), jnp.bfloat16),
        in_specs=[pl.BlockSpec(memory_space=pltpu.SMEM), whole, whole],
        out_specs=whole,
        compiler_params=pltpu.CompilerParams(vmem_limit_bytes=16 * 2**20),
    )(lengths, first, second)


def finish_kernel(
    arrived, param, mom, first, second, new_param, new_mom, new_first, new_second
):
    _, _, odd, _ = place()
    h, c = lax.axis_index("h"), lax.axis_index("c")
    for yl in range(2):
        columns = slice(yl * BLOCK, (yl + 1) * BLOCK)
        total = jnp.zeros((32, BLOCK), jnp.float32)
        for group in range(4):
            yh = lax.rem(h + odd, 2)
            source = group // 2 * 16 + c * 8 + yh * 4 + yl * 2 + group % 2
            total += arrived[source, 0].astype(jnp.float32)
        pseudo = total / 4
        momentum = 0.9 * mom[:, columns] + pseudo
        new_mom[:, columns] = momentum
        new_param[:, columns] = param[:, columns] - 0.7 * (pseudo + 0.9 * momentum)
    for block in range(8):
        fh, core, fl = block // 4, block // 2 % 2, block % 2
        columns = slice(block * BLOCK, (block + 1) * BLOCK)
        source = h * 16 + core * 8 + lax.rem(fh + odd, 2) * 4 + fl * 2 + c
        moments = first[0, :, columns], second[0, :, columns]
        for step in range(STEPS):
            grad = arrived[source, 1 + step].astype(jnp.float32)
            moments = adam_moments(*moments, grad)
        new_first[0, :, columns], new_second[0, :, columns] = moments


def finish(*arrays):
    whole = pl.BlockSpec(memory_space=pltpu.VMEM)
    return pl.pallas_call(
        finish_kernel,
        out_shape=[jax.ShapeDtypeStruct(a.shape, a.dtype) for a in arrays[1:]],
        in_specs=[whole] * 5,
        out_specs=[whole] * 4,
        compiler_params=pltpu.CompilerParams(vmem_limit_bytes=16 * 2**20),
    )(*arrays)


def product_kernel(layout, last, core, weights, *refs):
    count = len(layout)
    blocks, refs = refs[:count], refs[count:]
    earlier, out, held, goals, total, sems = refs if len(refs) == 6 else (None, *refs)
    copies, row = [], 0
    for at, (rows, inputs_at, goals_at) in enumerate(layout):
        half = pl.multiple_of(goals_at + core[0] * BLOCK, BLOCK)
        sources = blocks[at].at[:, pl.ds(inputs_at, D)], blocks[at].at[:, pl.ds(half, BLOCK)]
        here = pl.ds(row, rows)
        for kind, (source, target) in enumerate(zip(sources, (held, goals))):
            copy = pltpu.make_async_copy(source, target.at[here], sems.at[kind, at])
            copy.start()
            copies.append(copy)
        row += rows
    if earlier is not None:
        total[...] = earlier[...]
    row = at = 0
    while at < count:
        size = 0
        while size < 512:
            copies[2 * at].wait()
            copies[2 * at + 1].wait()
            size += layout[at][0]
            at += 1
        inputs = held[row : row + size]
        goal = goals[row : row + size].astype(jnp.float32)
        outputs = jnp.dot(inputs, weights[...], preferred_element_type=jnp.float32)
        resid = (outputs * D ** (-0.5) - goal).astype(jnp.bfloat16)
        grad = lax.dot_general(
            resid, inputs, (((0,), (0,)), ((), ())), preferred_element_type=jnp.float32
        )
        if row == 0 and earlier is None:
            total[...] = grad
        else:
            total[...] += grad
        row += size
    if last:
        for z in range(8):
            out[z] = total[:, z * 256 : (z + 1) * 256].T.astype(jnp.bfloat16)
    else:
        out[...] = total[...]


def product(parts, core, weights, earlier=None, last=False):
    blocks = [block for block, _, _ in parts]
    layout = [(block.shape[0], *places) for block, *places in parts]
    rows = sum(block.shape[0] for block in blocks)
    whole = pl.BlockSpec(memory_space=pltpu.VMEM)
    args = [core, weights, *blocks]
    specs = [pl.BlockSpec(memory_space=pltpu.SMEM), whole]
    specs += [pl.BlockSpec(memory_space=pl.ANY)] * len(blocks)
    if earlier is not None:
        args.append(earlier)
        specs.append(whole)
    shape = ((8, 256, BLOCK), jnp.bfloat16) if last else ((BLOCK, D), jnp.float32)
    return pl.pallas_call(
        functools.partial(product_kernel, layout, last),
        out_shape=jax.ShapeDtypeStruct(*shape),
        in_specs=specs,
        out_specs=whole,
        scratch_shapes=[
            pltpu.VMEM((rows, D), jnp.bfloat16),
            pltpu.VMEM((rows, BLOCK), jnp.bfloat16),
            pltpu.VMEM((BLOCK, D), jnp.float32),
            pltpu.SemaphoreType.DMA((2, len(blocks))),
        ],
        compiler_params=pltpu.CompilerParams(vmem_limit_bytes=40 * 2**20),
        cost_estimate=pl.CostEstimate(
            flops=8 * rows * D * BLOCK, bytes_accessed=2 * rows * D, transcendentals=0
        ),
    )(*args)


def among_peers(x):
    axes = ("z", "yh", "yl")
    return lax.all_to_all(x, axes, 0, 0, axis_index_groups=PEERS, tiled=True)


def gathered(param):
    weights = jnp.broadcast_to(param.astype(jnp.bfloat16)[None], (8, 256, BLOCK))
    return among_peers(weights).reshape(D, BLOCK)


def reduced(grad):
    return jnp.sum(among_peers(grad).astype(jnp.float32), 0)


def per_device(tokens, targets, lengths, outer_param, outer_mom, first_mom, second_mom):
    c, x = lax.axis_index("c"), lax.axis_index("x")
    _, _, odd, colour = place()
    core = c.reshape(1).astype(jnp.int32)

    half = tokens.shape[1] // 2
    mine_a = turned(prepare(0, lengths, tokens, targets))
    start = exchange(pack(outer_param), ("h", "yh", "yl", "x"))
    mine_b = turned(prepare(half, lengths, tokens, targets))

    def both(*columns):
        return jnp.concatenate([mine_a[:, slice(*columns)], mine_b[:, slice(*columns)]], 0)

    below, above = up(both(0, D + WIDE)), down(both(WIDE, D + 2 * WIDE))

    def plane_of(mine):
        wanted = mine[:, D + 2 * WIDE : D + 3 * WIDE]
        return jnp.concatenate([mine[:, WIDE : WIDE + D], wanted], 1)

    start = start.reshape(2, 256, BLOCK)
    here = pick(start, colour // 2, 0)
    there = pick(start, 1 - colour // 2, 0)
    weights = jnp.where(
        (jnp.arange(8) % 2 == odd)[:, None, None], here[None], there[None]
    )
    weights = exchange(weights, "z").reshape(D, BLOCK)
    start = here.astype(jnp.float32)
    mine_a, mine_b, weights = together(mine_a, mine_b, weights)
    before, behind = plane_of(mine_a), plane_of(mine_b)
    before, behind = shift(before, "z", 1), shift(behind, "z", -1)

    moments, weights = together(pack_moments(lengths, first_mom, second_mom), weights)
    moments = exchange(moments, ("c", "yh", "yl", "x"))
    moments, held = together(moments, mine_b)
    moments = pick(moments.reshape(2, 8, 80, BLOCK), x, 0)

    near = [(block, WIDE, D + 3 * WIDE) for block in (mine_a, mine_b)]
    near += [(other_core(block), WIDE, D + 3 * WIDE) for block in (mine_a, held)]
    near += [
        (block, 0, D)
        for block in (before, behind, other_core(before), other_core(behind))
    ]
    sides = [(block, WIDE, 0) for block in (below, other_core(below))]
    sides += [(block, 0, D) for block in (above, other_core(above))]
    grad = product(near, core, weights)
    grad = product(sides, core, weights, grad, last=True)

    first = moments[:, :32].reshape(256, BLOCK).astype(jnp.float32)
    second = moments[:, 32:64].reshape(256, BLOCK).astype(jnp.float32)
    coef = D ** (-0.5) / (128.0 * moments[0, 64, 0].astype(jnp.float32))
    grad = reduced(grad) * coef
    grads = [grad]
    first, second = adam_moments(first, second, grad)
    param = adam_update(start, first, second, PRIOR + 1)

    grad = product(near + sides, core, gathered(param), last=True)
    grad = reduced(grad) * coef
    grads.append(grad)
    first, second = adam_moments(first, second, grad)
    param = adam_update(param, first, second, PRIOR + 2)

    leaving = jnp.stack([start - param, *grads]).astype(jnp.bfloat16)
    leaving = jnp.moveaxis(leaving.reshape(3, 8, 32, BLOCK), 1, 0)
    leaving = jnp.broadcast_to(leaving[None], (4, 8, 3, 32, BLOCK))
    arrived = exchange(leaving.reshape(32, 3, 32, BLOCK), ("h", "c", "yh", "yl", "x"))
    return tuple(finish(arrived, outer_param, outer_mom, first_mom, second_mom))


def solution(mesh):
    fine = Mesh(
        mesh.devices.reshape(2, 2, 8, 2, 2, 2), ("h", "c", "z", "yh", "yl", "x")
    )
    group, fsdp = ("h", "c"), ("z", "yh", "yl", "x")
    in_specs = (
        P(group, fsdp, None),
        P(group, fsdp, None),
        P(group, None),
        P(fsdp, group),
        P(fsdp, group),
        P(group, fsdp, None),
        P(group, fsdp, None),
    )
    out_specs = (
        P(fsdp, group),
        P(fsdp, group),
        P(group, fsdp, None),
        P(group, fsdp, None),
    )
    return jax.shard_map(
        per_device, mesh=fine, in_specs=in_specs, out_specs=out_specs, check_vma=False
    )
```
